256 devices in a mesh: user: 4 (over x), seq: 64 (over z, y, core).
Axes of the slice: x: 4, y: 4, z: 8, core: 2. Of those that a mesh axis runs over, the one named last changes fastest.
Arguments:
- interaction_memory: bfloat16 [8, 32768, 1024], P('user', 'seq'), may hold values from -6 to 6
- contender_embeddings: bfloat16 [8, 8192, 1024], P('user', 'seq'), may hold values from -6 to 6
- contender_projection_matrix: bfloat16 [1024, 2048], replicated, may hold values from -0.1875 to 0.1875
- memory_projection_matrix: bfloat16 [1024, 2048], P(None, 'user'), may hold values from -0.1875 to 0.1875
- coarse_projection_matrix: bfloat16 [1024, 1024], replicated, may hold values from -0.1875 to 0.1875
- averaged_memory_matrix: bfloat16 [1024, 512], replicated, may hold values from -0.1875 to 0.1875
- finalist_indices: int32 [8, 256], P('user'), may hold values from -1 to 8191, as said below
- memory_extents: int32 [8], P('user'), may hold values from 2048 to 32768
Outputs:
- coarse_ratings: float32 [8, 8192], P('user', 'seq')
- fine_layer_result: bfloat16 [8, 8192, 1024], P('user', 'seq')
The draws below stay inside these ranges and needn't reach their ends.
Inputs may be any that keep to these rules, and one draw needn't show every extreme that they name: `finalist_indices`: within a user the indices are distinct. At most 8 of one user's survivors lie among the 128 candidates of one index of seq, and exactly 8 do for some index, for every user. For every even index i of seq, at most 8 of one user's survivors lie among the candidates of indices i and i + 1 together.
All inputs are finite; a program needn't handle non-finite values.
Results may differ from the reference program's by a relative error of at most 0.0036.
Values may be sent and summed in bfloat16 or wider, within the bound.
A program may use at most 64 MiB of HBM per device.

```python
import math
import jax
import jax.numpy as jnp
from jax import lax

DR = 1024
HEADS = 16
DP = 512
HIST_DEV = 512
CAND_DEV = 128
USERS = 8
HIST = 32768
CAND = 8192
SURV = 256
N_SEQ = 64


def draw_memory_extents(key, part):
    key = jax.random.fold_in(key, 11)
    key = jax.random.fold_in(key, part)
    keys = jax.random.split(key, 3)
    values = jax.random.randint(keys[0], (USERS,), HIST // 16, HIST + 1)
    longest = jax.random.randint(keys[1], (), 0, USERS)
    shortest = (longest + jax.random.randint(keys[2], (), 1, USERS)) % USERS
    values = values.at[longest].set(HIST)
    values = values.at[shortest].set(HIST // 16)
    return values.astype(jnp.int32)


def draw_finalist_indices(key, part):
    key = jax.random.fold_in(key, 23)
    holding_participants = CAND // CAND_DEV
    per_owner = SURV // holding_participants
    most = 2 * per_owner
    pairs = holding_participants // 2

    def one_member(member_key, member):
        keys = jax.random.split(member_key, 7)
        lift = jax.random.randint(keys[1], (pairs,), 0, per_owner + 1)
        capped = jax.random.randint(keys[5], (), 0, pairs)
        capped = jnp.where(member == 0, 0, capped)
        lift = lift.at[capped].set(per_owner)
        flips = jax.random.randint(keys[6], (pairs,), 0, 2)
        high_ids = 2 * jnp.arange(pairs) + flips
        low_ids = 2 * jnp.arange(pairs) + 1 - flips
        counts = jnp.zeros((holding_participants,), jnp.int32)
        counts = counts.at[high_ids].set(per_owner + lift)
        counts = counts.at[low_ids].set(per_owner - lift)
        lowered = jax.random.randint(keys[2], (holding_participants,), 0, 2)
        lowered = jnp.where(member == 0, jnp.ones_like(lowered), lowered)
        lowered = lowered.at[high_ids[capped]].set(0)
        lowered = lowered.at[low_ids[capped]].set(0)
        counts = jnp.maximum(counts - lowered, 0)
        raised = counts.at[holding_participants - 1].set(jnp.maximum(counts[holding_participants - 1], 1))
        counts = jnp.where(member == 0, raised, counts)
        shuffles = jax.vmap(lambda inner: jax.random.permutation(inner, CAND_DEV))(jax.random.split(keys[3], holding_participants))
        last_row = shuffles[holding_participants - 1]
        turned = (last_row + (CAND_DEV - 1 - last_row[0])) % CAND_DEV
        shuffles = jnp.where(member == 0, shuffles.at[holding_participants - 1].set(turned), shuffles)
        picks = shuffles[:, :most]
        ranks = jnp.arange(most)
        valid = ranks[None, :] < counts[:, None]
        ids = jnp.arange(holding_participants)[:, None] * CAND_DEV + picks
        flat_ids = jnp.where(valid, ids, -1).reshape(-1)
        flat_valid = valid.reshape(-1).astype(jnp.int32)
        placed = jnp.argsort(1 - flat_valid, stable=True)[:SURV]
        chosen_ids = flat_ids[placed]
        return chosen_ids[jax.random.permutation(keys[4], SURV)]
    member_keys = jax.random.split(key, USERS)
    return jax.vmap(one_member)(member_keys, jnp.arange(USERS)).astype(jnp.int32)


def block_levels(rng, shape, shards, smallest, high):
    loudness, own = 1.0, jax.random.fold_in(rng, 6)
    for dim, shards_of in shards:
        heights = jnp.exp(jax.random.uniform(jax.random.fold_in(own, dim), (shards_of,), jnp.float32, smallest / len(shards), high / len(shards)))
        loudness = loudness * jnp.repeat(heights, shape[dim] // shards_of).reshape([-1 if axis == dim else 1 for axis in range(len(shape))])
    return loudness


def bell_draw(own_key, extent, deviation, reach, shards=(), kind=jnp.bfloat16):
    level = block_levels(own_key, extent, shards, -0.22, 0.18) if shards else 1.0
    drawn = jax.random.normal(own_key, extent, jnp.float32) * deviation * level
    return jnp.minimum(jnp.maximum(drawn, -reach), reach).astype(kind)


def setup_inputs(seed: int = 0) -> dict:
    streams_of = jax.random.split(jax.random.key(seed), 9)
    interaction_memory = bell_draw(streams_of[0], (USERS, HIST, DR), 1.0, 6.0, ((0, 4), (1, 64)))
    contender_embeddings = bell_draw(streams_of[1], (USERS, CAND, DR), 1.0, 6.0, ((0, 4), (1, 64)))
    contender_projection_matrix = bell_draw(streams_of[2], (DR, 2 * DR), DR ** -0.5, 0.1875)
    memory_projection_matrix = bell_draw(streams_of[3], (DR, 2 * DR), DR ** -0.5, 0.1875, ((1, 4),))
    coarse_projection_matrix = bell_draw(streams_of[4], (DR, 2 * DP), DR ** -0.5, 0.1875)
    averaged_memory_matrix = bell_draw(streams_of[5], (DR, DP), DR ** -0.5, 0.1875)
    finalist_indices = draw_finalist_indices(jax.random.fold_in(streams_of[8], 71), 0)
    memory_extents = draw_memory_extents(jax.random.fold_in(streams_of[8], 71), 0)
    return dict(interaction_memory=interaction_memory, contender_embeddings=contender_embeddings, contender_projection_matrix=contender_projection_matrix, memory_projection_matrix=memory_projection_matrix, coarse_projection_matrix=coarse_projection_matrix, averaged_memory_matrix=averaged_memory_matrix, finalist_indices=finalist_indices, memory_extents=memory_extents)


epsilon = 1e-05

def reference(interaction_memory, contender_embeddings, contender_projection_matrix, memory_projection_matrix, coarse_projection_matrix, averaged_memory_matrix, finalist_indices, memory_extents):
    head_dim = DR // HEADS

    def participant_portion(items):
        hist_rows, contender_entries, chosen_ids, length = items
        live = (jnp.arange(HIST) < length).astype(jnp.float32)
        column_sum = jnp.dot(live.astype(jnp.bfloat16), hist_rows, preferred_element_type=jnp.float32)
        pooled = jnp.dot(column_sum, averaged_memory_matrix.astype(jnp.float32), precision=lax.Precision.HIGHEST)
        pooled = pooled / jnp.sqrt(length.astype(jnp.float32))
        gate_up = jnp.dot(contender_entries, coarse_projection_matrix, preferred_element_type=jnp.float32)
        pre_hidden = jax.nn.silu(gate_up[:, :DP]) * gate_up[:, DP:]
        scores = jnp.dot(pre_hidden, pooled, precision=lax.Precision.HIGHEST) / math.sqrt(DP)
        projected = jnp.dot(hist_rows, memory_projection_matrix, preferred_element_type=jnp.float32)
        keys = jax.nn.silu(projected[:, :DR]).astype(jnp.bfloat16)
        values = projected[:, DR:].astype(jnp.bfloat16)
        valid = chosen_ids >= 0
        rows = contender_entries[jnp.where(valid, chosen_ids, 0)]
        rows = jnp.where(valid[:, None], rows, jnp.zeros_like(rows))
        lifted = jax.nn.silu(jnp.dot(rows, contender_projection_matrix, preferred_element_type=jnp.float32))
        gates = lifted[:, :DR]
        queries = lifted[:, DR:].astype(jnp.bfloat16)
        query_heads = queries.astype(jnp.float32).reshape(SURV, HEADS, head_dim)
        key_blocks = keys.reshape(N_SEQ, HIST_DEV, HEADS, head_dim)
        value_blocks = values.reshape(N_SEQ, HIST_DEV, HEADS, head_dim)
        live_blocks = live.reshape(N_SEQ, HIST_DEV)

        def step(total, block):
            key_block, value_block, live_block = block
            logits = jnp.einsum('rhd,jhd->hrj', query_heads, key_block.astype(jnp.float32)) / math.sqrt(head_dim)
            weights = (jax.nn.silu(logits) * live_block[None, None, :]).astype(jnp.bfloat16)
            added = jnp.einsum('hrj,jhd->rhd', weights.astype(jnp.float32), value_block.astype(jnp.float32))
            return (total + added, None)
        attention, _ = lax.scan(step, jnp.zeros((SURV, HEADS, head_dim), jnp.float32), (key_blocks, value_blocks, live_blocks))
        attention = attention.reshape(SURV, DR)
        mean = lax.optimization_barrier(jnp.mean(attention, axis=-1, keepdims=True))
        centred = attention - mean
        variance = lax.optimization_barrier(jnp.mean(centred * centred, axis=-1, keepdims=True))
        normed = centred / jnp.sqrt(variance + epsilon)
        mixed = (normed * gates + rows.astype(jnp.float32)).astype(jnp.bfloat16)
        target = jnp.where(valid, chosen_ids, CAND).astype(jnp.int32)
        placed = jnp.zeros((CAND, DR), jnp.bfloat16).at[target].set(mixed, mode='drop')
        return (scores, placed)
    coarse_ratings, fine_layer_result = lax.map(participant_portion, (interaction_memory, contender_embeddings, finalist_indices, memory_extents))
    return (coarse_ratings, fine_layer_result)
```

```python
import functools
import math

import jax
import jax.numpy as jnp
from jax import lax
from jax.experimental import pallas as pl
from jax.experimental.pallas import tpu as pltpu
from jax.sharding import PartitionSpec as P

HEADS = 16
CORES = 2
YS = 4
XS = 4
CHUNKS = 4
LANES = 128
SLOTS = 8
epsilon = 1e-05

F32 = jnp.float32
BF16 = jnp.bfloat16
MESH = pl.DeviceIdType.MESH


def dot(a, b):
    return jnp.dot(a, b, preferred_element_type=F32)


def dot_nt(a, b):
    return lax.dot_general(a, b, (((1,), (1,)), ((), ())), preferred_element_type=F32)


def silu(x):
    h = x * 0.5
    return h + h * jnp.tanh(h)


def kernel(
    zs,
    m_hbm, cand_hbm, wc_hbm, wm_hbm, wco_hbm, avg_hbm, idx_ref, ext_ref,
    coarse_ref, fine_ref,
    cand, wq, wg, wco, avg, mall, wbuf,
    xbuf, xrow, gates, sel, selt,
    qbuf, q2, kbuf, vbuf, pf, psend, pown, yrecv, zown, zsend, zrecv, afull,
    pre, cs, csy, csz, pool,
    local_sem, wl_sem, m_sem, x_sem, wx_send, wx_recv, wf_send, wf_recv,
    qz_send, qz_recv, qy_send, qy_recv,
    cy_send, cy_recv, cz_send, cz_recv, cp_sem,
    py_send, py_recv, pz_send, pz_recv, a_sem,
):
    u = lax.axis_index("user")
    s = lax.axis_index("seq")
    c = s % CORES
    y = (s // CORES) % YS
    z = s // (CORES * YS)
    chip = s // CORES
    hist = m_hbm.shape[1]
    half = wq.shape[1]
    colour = (y + 2 * z) % CHUNKS

    def at(x_, z_, y_, c_):
        return (x_, (z_ * YS + y_) * CORES + c_)

    sibling = at(u, z, y, 1 - c)

    def xpeer(d):
        return at((u + d) % XS, z, y, c)

    def ypeer(d):
        return at(u, z, (y + d) % YS, c)

    def zpeer(d):
        return at(u, (z + d) % zs, y, c)

    def lanes(start, size):
        return pl.ds(pl.multiple_of(start, LANES), size)

    def remote(src, dst, send, recv, device):
        return pltpu.make_async_remote_copy(
            src_ref=src, dst_ref=dst, send_sem=send, recv_sem=recv,
            device_id=device, device_id_type=MESH,
        )

    l_cand = pltpu.make_async_copy(cand_hbm, cand, local_sem.at[0])
    l_wq = pltpu.make_async_copy(
        wc_hbm.at[:, lanes(2 * half + c * half, half)], wq, local_sem.at[1]
    )
    l_m = pltpu.make_async_copy(m_hbm, mall.at[c], local_sem.at[2])
    l_wg = pltpu.make_async_copy(wc_hbm.at[:, pl.ds(0, 2 * half)], wg, local_sem.at[3])
    l_wco = pltpu.make_async_copy(wco_hbm, wco, local_sem.at[4])
    l_avg = pltpu.make_async_copy(
        avg_hbm.at[pl.ds(pl.multiple_of(c * half, half), half), :], avg, local_sem.at[5]
    )
    l_cand.start()
    l_wq.start()

    barrier = pltpu.get_barrier_semaphore()

    def greet(device):
        pl.semaphore_signal(barrier, inc=1, device_id=device, device_id_type=MESH)

    greet(sibling)
    for d in range(1, XS):
        greet(xpeer(d))
    for d in range(1, YS):
        greet(ypeer(d))
    for d in range(1, zs):
        greet(zpeer(d))

    l_m.start()
    l_wg.start()
    l_wco.start()
    l_avg.start()

    own_kv = u // 2
    holds = (u % 2) == c

    def wl_copy(q):
        return pltpu.make_async_copy(
            wm_hbm.at[:, lanes(q * LANES, LANES)], wbuf.at[q, own_kv], wl_sem.at[q]
        )

    @pl.when(holds)
    def _():
        for q in range(CHUNKS):
            wl_copy(q).start()

    rows16 = 2 * SLOTS
    ones = jnp.ones((rows16, idx_ref.shape[1]), BF16)
    pair = 2 * cand_hbm.shape[1]
    mine = cand_hbm.shape[1]
    upper = jnp.where(
        lax.broadcasted_iota(jnp.int32, (pair, pair), 0)
        < lax.broadcasted_iota(jnp.int32, (pair, pair), 1),
        1.0, 0.0,
    ).astype(BF16)
    eye = jnp.where(
        lax.broadcasted_iota(jnp.int32, (mine, mine), 0)
        == lax.broadcasted_iota(jnp.int32, (mine, mine), 1),
        1.0, 0.0,
    ).astype(BF16)
    row = lax.broadcasted_iota(jnp.int32, (rows16, pair), 0)
    for b in range(2):
        near = idx_ref[b:b + 1, :] - chip * pair
        matches = jnp.where(
            lax.broadcasted_iota(jnp.int32, (pair, idx_ref.shape[1]), 0) == near, 1.0, 0.0
        ).astype(BF16)
        flagged = dot_nt(ones, matches)
        placing = dot(flagged.astype(BF16), upper)
        target = (row - b * SLOTS).astype(F32)
        chosen = jnp.where((flagged > 0.5) & (jnp.abs(placing - target) < 0.5), 1.0, 0.0)
        chosen = jnp.where((row // SLOTS) == b, chosen, 0.0)
        own = jnp.where(c == 0, chosen[:, :mine], chosen[:, mine:]).astype(BF16)
        sel[b] = own
        selt[b] = dot_nt(eye, own).astype(BF16)

    l_cand.wait()
    found = dot(sel[0], cand[0]) + dot(sel[1], cand[1])
    xrow[...] = found.astype(BF16)

    pl.semaphore_wait(barrier, 1 + (XS - 1) + (YS - 1) + (zs - 1))

    x_copy = remote(xrow, xbuf, x_sem.at[0], x_sem.at[1], sibling)
    x_copy.start()

    def wx_copy(d):
        return remote(
            wm_hbm.at[:, lanes(colour * LANES, LANES)], wbuf.at[colour, own_kv],
            wx_send.at[d - 1], wx_recv.at[own_kv], xpeer(d),
        )

    @pl.when(holds)
    def _():
        for d in (1, 3, 2):
            wx_copy(d).start()

    x_copy.wait_recv()
    rows = xrow[...].astype(F32) + xbuf[...].astype(F32)
    xrow2 = rows.astype(BF16)
    l_wq.wait()
    queries = silu(dot(xrow2, wq[...])).astype(BF16)
    qbuf[y, z] = (queries.astype(F32) * (0.5 / math.sqrt(2 * half // HEADS))).astype(BF16)

    def qz_copy(d):
        return remote(qbuf.at[y, z], qbuf.at[y, z], qz_send.at[d - 1], qz_recv.at[d - 1], zpeer(d))

    for d in range(1, zs):
        qz_copy(d).start()
    m_copy = remote(m_hbm, mall.at[c], m_sem.at[0], m_sem.at[1], sibling)
    m_copy.start()

    l_wg.wait()
    gates[...] = silu(dot(xrow2, wg[...]))

    depth = wbuf.shape[2] // 2

    def wf_copies(kv):
        block = wbuf.at[colour, kv]
        low = wbuf.at[colour, kv, pl.ds(0, depth)]
        high = wbuf.at[colour, kv, pl.ds(depth, depth)]
        return (
            remote(block, block, wf_send.at[kv, 0], wf_recv.at[kv, 0], ypeer(1)),
            remote(block, block, wf_send.at[kv, 1], wf_recv.at[kv, 1], ypeer(YS - 1)),
            remote(low, low, wf_send.at[kv, 2], wf_recv.at[kv, 2], zpeer(1)),
            remote(high, high, wf_send.at[kv, 3], wf_recv.at[kv, 3], zpeer(zs - 1)),
        )

    def wx_wait(kv):
        block = wbuf.at[colour, kv]
        remote(block, block, wx_send.at[0], wx_recv.at[kv], xpeer(1)).wait_recv()

    def forward(kv):
        @pl.when(c + 2 * kv != u)
        def _():
            wx_wait(kv)
            for copy in wf_copies(kv):
                copy.start()

    forward(0)
    forward(1)

    for d in range(1, zs):
        qz_copy(d).wait_recv()

    def qy_copy(d):
        return remote(qbuf.at[y], qbuf.at[y], qy_send.at[d - 1], qy_recv.at[d - 1], ypeer(d))

    for d in range(1, YS):
        qy_copy(d).start()

    l_wco.wait()
    for b in range(2):
        hidden = dot(cand[b], wco[...])
        pre[b] = silu(hidden[:, :half]) * hidden[:, half:]

    l_m.wait()
    m_copy.wait_recv()
    live_row = lax.broadcasted_iota(jnp.int32, (rows16, hist), 0)
    live_col = lax.broadcasted_iota(jnp.int32, (rows16, hist), 1)
    total = jnp.zeros((rows16, half), F32)
    for b in range(2):
        for core in range(CORES):
            place = (chip * CORES + core) * hist + live_col
            mask = jnp.where((live_row == b) & (place < ext_ref[b]), 1.0, 0.0).astype(BF16)
            total = total + dot(mask, mall[core, b, :, lanes(c * half, half)])
    cs[0] = total[:8]

    def cy_copy(d):
        return remote(cs.at[0], csy.at[d - 1], cy_send.at[d - 1], cy_recv.at[d - 1], ypeer(d))

    def cz_copy(d):
        return remote(cs.at[1], csz.at[d - 1], cz_send.at[d - 1], cz_recv.at[d - 1], zpeer(d))

    for d in range(1, YS):
        cy_copy(d).start()

    for d in range(1, YS):
        qy_copy(d).wait_recv()
    for yy in range(YS):
        block = qbuf[yy].astype(F32)
        for b in range(2):
            part = block[:, b * SLOTS:(b + 1) * SLOTS, :].reshape(zs * SLOTS, half)
            q2[b, yy * zs * SLOTS:(yy + 1) * zs * SLOTS, :] = part.astype(BF16)

    for d in range(1, YS):
        cy_copy(d).wait_recv()
    cs[1] = cs[0] + (csy[0] + csy[1] + csy[2])
    for d in range(1, zs):
        cz_copy(d).start()

    def py_copy(q, d):
        return remote(
            psend.at[q, (y + d) % YS], yrecv.at[q, d - 1],
            py_send.at[q, d - 1], py_recv.at[q, d - 1], ypeer(d),
        )

    def pz_copy(q, d):
        return remote(
            zsend.at[q, (z + d) % zs], zrecv.at[q, d - 1],
            pz_send.at[q, d - 1], pz_recv.at[q, d - 1], zpeer(d),
        )

    lane = lax.broadcasted_iota(jnp.int32, (YS * zs * SLOTS, LANES), 1)
    first = lane < (LANES // 2)
    spot = lax.broadcasted_iota(jnp.int32, (hist, LANES), 0)

    def w_wait(q, kv):
        near = (q - colour + CHUNKS) % CHUNKS
        local_ = c + 2 * kv == u

        @pl.when(local_)
        def _():
            wl_copy(q).wait()

        @pl.when(jnp.logical_not(local_))
        def _():
            copies = wf_copies(kv)

            @pl.when(near == 1)
            def _():
                copies[1].wait_recv()

            @pl.when(near == 3)
            def _():
                copies[0].wait_recv()

            @pl.when(near == 2)
            def _():
                copies[2].wait_recv()
                copies[3].wait_recv()

    def compute(q):
        w_wait(q, 0)
        w_wait(q, 1)

        def project(i, carry):
            b, core = i // CORES, i % CORES
            weights = jnp.concatenate([wbuf[q, 0], wbuf[q, 1]], axis=1)
            raw = dot(mall[core, b], weights)
            at_rows = pl.ds(pl.multiple_of(core * hist, hist), hist)
            kbuf[b, at_rows, :] = silu(raw[:, :LANES]).astype(BF16)
            place = (chip * CORES + core) * hist + spot
            vbuf[b, at_rows, :] = jnp.where(place < ext_ref[b], raw[:, LANES:], 0.0).astype(BF16)
            return carry

        lax.fori_loop(0, 2 * CORES, project, 0)

        for b in range(2):
            queries_ = q2[b, :, lanes(q * LANES, LANES)]
            outs = []
            for h in range(2):
                keep = first if h == 0 else jnp.logical_not(first)
                masked = jnp.where(keep, queries_.astype(F32), 0.0).astype(BF16)
                logits = dot_nt(masked, kbuf[b])
                weights = (logits + logits * jnp.tanh(logits)).astype(BF16)
                outs.append(dot(weights, vbuf[b]))
            out = jnp.where(first, outs[0], outs[1])
            pf[:, :, b * SLOTS:(b + 1) * SLOTS, :] = out.reshape(YS, zs, SLOTS, LANES)
        psend[q] = pf[...].astype(BF16)
        pown[q] = pf[y]
        for d in range(1, YS):
            py_copy(q, d).start()

    def reduce_y(q):
        for d in range(1, YS):
            py_copy(q, d).wait_recv()
        total_ = pown[q]
        for d in range(1, YS):
            total_ = total_ + yrecv[q, d - 1].astype(F32)
        pown[q] = total_
        zsend[q] = total_.astype(BF16)
        zown[q] = pown[q, z]
        for d in range(1, zs):
            pz_copy(q, d).start()

    def step(q, carry):
        @pl.when(q < CHUNKS)
        def _():
            compute(q)

        @pl.when(q > 0)
        def _():
            reduce_y(q - 1)

        return carry

    lax.fori_loop(0, CHUNKS + 1, step, 0)

    for d in range(1, zs):
        cz_copy(d).wait_recv()
    summed = cs[1]
    for d in range(1, zs):
        summed = summed + csz[d - 1]
    l_avg.wait()
    part1 = summed.astype(BF16)
    rest = summed - part1.astype(F32)
    part2 = rest.astype(BF16)
    part3 = (rest - part2.astype(F32)).astype(BF16)
    pool[0] = dot(part1, avg[...]) + dot(part2, avg[...]) + dot(part3, avg[...])
    cp_copy = remote(pool.at[0], pool.at[1], cp_sem.at[0], cp_sem.at[1], sibling)
    cp_copy.start()

    def reduce_z(q, carry):
        total_ = zown[q]
        for d in range(1, zs):
            pz_copy(q, d).wait_recv()
            total_ = total_ + zrecv[q, d - 1].astype(F32)
        afull[c, q] = total_
        return carry

    lax.fori_loop(0, CHUNKS, reduce_z, 0)
    a_copy = remote(afull.at[c], afull.at[c], a_sem.at[0], a_sem.at[1], sibling)
    a_copy.start()

    cp_copy.wait_recv()
    pooled = pool[0] + pool[1]
    for b in range(2):
        scale = 1.0 / (
            jnp.sqrt(jnp.full((8, LANES), ext_ref[b], jnp.int32).astype(F32)) * math.sqrt(half)
        )
        scores = lax.dot_general(
            pooled, pre[b], (((1,), (1,)), ((), ())),
            precision=lax.Precision.HIGHEST, preferred_element_type=F32,
        )
        coarse_ref[b:b + 1, :] = (scores * scale)[b:b + 1, :]

    a_copy.wait_recv()
    attention = jnp.concatenate(
        [afull[core, q] for core in range(CORES) for q in range(CHUNKS)], axis=1
    )
    width = 2 * half
    mean = jnp.sum(attention, axis=-1, keepdims=True) * (1.0 / width)
    centred = attention - mean
    variance = jnp.sum(centred * centred, axis=-1, keepdims=True) * (1.0 / width)
    normed = centred / jnp.sqrt(variance + epsilon)
    chosen_rows = xrow[...].astype(F32) + xbuf[...].astype(F32)
    mixed = (normed * gates[...] + chosen_rows).astype(BF16)
    for b in range(2):
        fine_ref[b] = dot(selt[b], mixed).astype(BF16)

    x_copy.wait_send()
    m_copy.wait_send()
    cp_copy.wait_send()
    a_copy.wait_send()

    @pl.when(holds)
    def _():
        for d in range(1, XS):
            wx_copy(d).wait_send()

    for kv in range(2):
        @pl.when(c + 2 * kv != u)
        def _():
            for copy in wf_copies(kv):
                copy.wait_send()

    for d in range(1, zs):
        qz_copy(d).wait_send()
        cz_copy(d).wait_send()
    for d in range(1, YS):
        qy_copy(d).wait_send()
        cy_copy(d).wait_send()

    def drain(q, carry):
        for d in range(1, YS):
            py_copy(q, d).wait_send()
        for d in range(1, zs):
            pz_copy(q, d).wait_send()
        return carry

    lax.fori_loop(0, CHUNKS, drain, 0)


def local(memory, contenders, wc, wm, wco, avg, idx, ext):
    users, hist, width = memory.shape
    entries = contenders.shape[1]
    half = width // 2
    zs = lax.axis_size("seq") // (CORES * YS)
    slots = YS * zs * SLOTS
    dma = pltpu.SemaphoreType.DMA
    vmem = pltpu.VMEM
    any_ = pl.BlockSpec(memory_space=pl.ANY)
    scratch = [
        vmem((users, entries, width), BF16),
        vmem((width, half), BF16),
        vmem((width, width), BF16),
        vmem((width, width), BF16),
        vmem((half, half), BF16),
        vmem((CORES, users, hist, width), BF16),
        vmem((CHUNKS, 2, width, LANES), BF16),
        vmem((2 * SLOTS, width), BF16),
        vmem((2 * SLOTS, width), BF16),
        vmem((2 * SLOTS, width), F32),
        vmem((users, 2 * SLOTS, entries), BF16),
        vmem((users, entries, 2 * SLOTS), BF16),
        vmem((YS, zs, 2 * SLOTS, half), BF16),
        vmem((users, slots, half), BF16),
        vmem((users, CORES * hist, LANES), BF16),
        vmem((users, CORES * hist, LANES), BF16),
        vmem((YS, zs, 2 * SLOTS, LANES), F32),
        vmem((CHUNKS, YS, zs, 2 * SLOTS, LANES), BF16),
        vmem((CHUNKS, zs, 2 * SLOTS, LANES), F32),
        vmem((CHUNKS, YS - 1, zs, 2 * SLOTS, LANES), BF16),
        vmem((CHUNKS, 2 * SLOTS, LANES), F32),
        vmem((CHUNKS, zs, 2 * SLOTS, LANES), BF16),
        vmem((CHUNKS, zs - 1, 2 * SLOTS, LANES), BF16),
        vmem((CORES, CHUNKS, 2 * SLOTS, LANES), F32),
        vmem((users, entries, half), F32),
        vmem((2, 8, half), F32),
        vmem((YS - 1, 8, half), F32),
        vmem((zs - 1, 8, half), F32),
        vmem((2, 8, half), F32),
        dma((6,)),
        dma((CHUNKS,)),
        dma((2,)),
        dma((2,)),
        dma((XS - 1,)),
        dma((2,)),
        dma((2, 4)),
        dma((2, 4)),
        dma((zs - 1,)),
        dma((zs - 1,)),
        dma((YS - 1,)),
        dma((YS - 1,)),
        dma((YS - 1,)),
        dma((YS - 1,)),
        dma((zs - 1,)),
        dma((zs - 1,)),
        dma((2,)),
        dma((CHUNKS, YS - 1)),
        dma((CHUNKS, YS - 1)),
        dma((CHUNKS, zs - 1)),
        dma((CHUNKS, zs - 1)),
        dma((2,)),
    ]
    return pl.pallas_call(
        functools.partial(kernel, zs),
        out_shape=(
            jax.ShapeDtypeStruct((users, entries), F32),
            jax.ShapeDtypeStruct((users, entries, width), BF16),
        ),
        in_specs=[any_] * 6
        + [pl.BlockSpec(memory_space=pltpu.VMEM), pl.BlockSpec(memory_space=pltpu.SMEM)],
        out_specs=(
            pl.BlockSpec(memory_space=pltpu.VMEM),
            pl.BlockSpec(memory_space=pltpu.VMEM),
        ),
        scratch_shapes=scratch,
        compiler_params=pltpu.CompilerParams(
            collective_id=0, has_side_effects=True, vmem_limit_bytes=56 * 1024 * 1024
        ),
        cost_estimate=pl.CostEstimate(
            flops=6_500_000_000, bytes_accessed=12_000_000, transcendentals=7_000_000
        ),
    )(memory, contenders, wc, wm, wco, avg, idx, ext)


def solution(mesh):
    placed = (
        P("user", "seq", None),
        P("user", "seq", None),
        P(),
        P(None, "user"),
        P(),
        P(),
        P("user", None),
        P("user"),
    )
    return jax.shard_map(
        local,
        mesh=mesh,
        in_specs=placed,
        out_specs=(P("user", "seq"), P("user", "seq", None)),
        check_vma=False,
    )
```

```python
import functools
import math

import jax
import jax.numpy as jnp
from jax import lax
from jax.experimental import pallas as pl
from jax.experimental.pallas import tpu as pltpu
from jax.sharding import PartitionSpec as P

HEADS = 16
CORES = 2
YS = 4
XS = 4
CHUNKS = 4
LANES = 128
SLOTS = 8
epsilon = 1e-05

F32 = jnp.float32
BF16 = jnp.bfloat16
MESH = pl.DeviceIdType.MESH


def dot(a, b):
    return jnp.dot(a, b, preferred_element_type=F32)


def dot_nt(a, b):
    return lax.dot_general(a, b, (((1,), (1,)), ((), ())), preferred_element_type=F32)


def silu(x):
    h = x * 0.5
    return h + h * jnp.tanh(h)


def kernel(
    zs,
    m_hbm, cand_hbm, wc_hbm, wm_hbm, wco_hbm, avg_hbm, idx_ref, ext_ref,
    coarse_ref, mixed_ref, selt,
    cand, wq, wg, wco, avg, mall, wbuf,
    xbuf, xrow, gates, sel,
    qbuf, q2, kbuf, vbuf, pf, psend, pown, yrecv, zown, zsend, zrecv, afull,
    pre, cs, csy, csz, pool,
    local_sem, wl_sem, m_sem, x_sem, wx_send, wx_recv, wh_send, wh_recv, wf_send, wf_recv,
    qz_send, qz_recv, qy_send, qy_recv,
    cy_send, cy_recv, cz_send, cz_recv, cp_sem,
    py_send, py_recv, pz_send, pz_recv, a_sem,
):
    u = lax.axis_index("user")
    s = lax.axis_index("seq")
    c = s % CORES
    y = (s // CORES) % YS
    z = s // (CORES * YS)
    chip = s // CORES
    hist = m_hbm.shape[1]
    half = wq.shape[1]
    colour = (y + z) % 2

    def at(x_, z_, y_, c_):
        return (x_, (z_ * YS + y_) * CORES + c_)

    sibling = at(u, z, y, 1 - c)

    def xpeer(d):
        return at((u + d) % XS, z, y, c)

    def ypeer(d):
        return at(u, z, (y + d) % YS, c)

    def zpeer(d):
        return at(u, (z + d) % zs, y, c)

    def lanes(start, size):
        return pl.ds(pl.multiple_of(start, LANES), size)

    def remote(src, dst, send, recv, device):
        return pltpu.make_async_remote_copy(
            src_ref=src, dst_ref=dst, send_sem=send, recv_sem=recv,
            device_id=device, device_id_type=MESH,
        )

    l_cand = pltpu.make_async_copy(cand_hbm, cand, local_sem.at[0])
    l_wq = pltpu.make_async_copy(
        wc_hbm.at[:, lanes(2 * half + c * half, half)], wq, local_sem.at[1]
    )
    l_m = pltpu.make_async_copy(m_hbm, mall.at[c], local_sem.at[2])
    l_wg = pltpu.make_async_copy(wc_hbm.at[:, pl.ds(0, 2 * half)], wg, local_sem.at[3])
    l_wco = pltpu.make_async_copy(wco_hbm, wco, local_sem.at[4])
    l_avg = pltpu.make_async_copy(
        avg_hbm.at[pl.ds(pl.multiple_of(c * half, half), half), :], avg, local_sem.at[5]
    )
    l_cand.start()
    l_wq.start()

    barrier = pltpu.get_barrier_semaphore()

    def greet(device):
        pl.semaphore_signal(barrier, inc=1, device_id=device, device_id_type=MESH)

    greet(sibling)
    for d in range(1, XS):
        greet(xpeer(d))
    for d in range(1, YS):
        greet(ypeer(d))
    for d in range(1, zs):
        greet(zpeer(d))

    l_m.start()
    l_wg.start()
    l_wco.start()
    l_avg.start()

    own_kv = u // 2
    holds = (u % 2) == c

    def wl_copy(q):
        return pltpu.make_async_copy(
            wm_hbm.at[:, lanes(q * LANES, LANES)], wbuf.at[q, own_kv], wl_sem.at[q]
        )

    @pl.when(holds)
    def _():
        for q in range(CHUNKS):
            wl_copy(q).start()

    rows16 = 2 * SLOTS
    ones = jnp.ones((rows16, idx_ref.shape[1]), BF16)
    pair = 2 * cand_hbm.shape[1]
    mine = cand_hbm.shape[1]
    upper = jnp.where(
        lax.broadcasted_iota(jnp.int32, (pair, pair), 0)
        < lax.broadcasted_iota(jnp.int32, (pair, pair), 1),
        1.0, 0.0,
    ).astype(BF16)
    eye = jnp.where(
        lax.broadcasted_iota(jnp.int32, (mine, mine), 0)
        == lax.broadcasted_iota(jnp.int32, (mine, mine), 1),
        1.0, 0.0,
    ).astype(BF16)
    row = lax.broadcasted_iota(jnp.int32, (rows16, pair), 0)
    for b in range(2):
        near = idx_ref[b:b + 1, :] - chip * pair
        matches = jnp.where(
            lax.broadcasted_iota(jnp.int32, (pair, idx_ref.shape[1]), 0) == near, 1.0, 0.0
        ).astype(BF16)
        flagged = dot_nt(ones, matches)
        placing = dot(flagged.astype(BF16), upper)
        target = (row - b * SLOTS).astype(F32)
        chosen = jnp.where((flagged > 0.5) & (jnp.abs(placing - target) < 0.5), 1.0, 0.0)
        chosen = jnp.where((row // SLOTS) == b, chosen, 0.0)
        own = jnp.where(c == 0, chosen[:, :mine], chosen[:, mine:]).astype(BF16)
        sel[b] = own
        selt[b] = dot_nt(eye, own).astype(BF16)

    l_cand.wait()
    found = dot(sel[0], cand[0]) + dot(sel[1], cand[1])
    xrow[...] = found.astype(BF16)

    pl.semaphore_wait(barrier, 1 + (XS - 1) + (YS - 1) + (zs - 1))

    x_copy = remote(xrow, xbuf, x_sem.at[0], x_sem.at[1], sibling)
    x_copy.start()

    m_copy = remote(m_hbm, mall.at[c], m_sem.at[0], m_sem.at[1], sibling)
    m_copy.start()

    depth = wbuf.shape[2] // 2

    def part(q, kv, high):
        return wbuf.at[q, kv, pl.ds(high * depth, depth)]

    def wx_copy(j, d):
        q = 2 * colour + j
        return remote(
            wm_hbm.at[:, lanes(q * LANES, LANES)], wbuf.at[q, own_kv],
            wx_send.at[j, d // 2], wx_recv.at[j, own_kv], xpeer(d),
        )

    @pl.when(holds)
    def _():
        for j in range(2):
            for d in (1, 3):
                wx_copy(j, d).start()

    def wh_copy(j, kv, high):
        half_ = part(2 * colour + j, kv, high)
        return remote(
            half_, half_, wh_send.at[j, high], wh_recv.at[j, high],
            xpeer(XS - 1 if high else 1),
        )

    def wf_copy(j, kv, high):
        half_ = part(2 * colour + j, kv, high)
        peer = ypeer if j == 0 else zpeer
        return remote(
            half_, half_, wf_send.at[j, kv, high], wf_recv.at[j, kv, high],
            peer((YS if j == 0 else zs) - 1 if high else 1),
        )

    def near_relay(j):
        @pl.when(jnp.logical_not(holds))
        def _():
            for kv in range(2):
                block = wbuf.at[2 * colour + j, kv]
                remote(
                    block, block, wx_send.at[j, 0], wx_recv.at[j, kv], xpeer(1)
                ).wait_recv()
                behind = (c + 2 * kv + 1) % XS == u

                @pl.when(behind)
                def _():
                    wh_copy(j, kv, 0).start()

                @pl.when(jnp.logical_not(behind))
                def _():
                    wh_copy(j, kv, 1).start()

            for kv in range(2):
                for high in range(2):
                    wf_copy(j, kv, high).start()

    def far_relay(j):
        @pl.when(holds)
        def _():
            for high in range(2):
                half_ = part(2 * colour + j, 1 - own_kv, high)
                remote(
                    half_, half_, wh_send.at[j, high], wh_recv.at[j, high], xpeer(1)
                ).wait_recv()
                wf_copy(j, 1 - own_kv, high).start()

    x_copy.wait_recv()
    rows = xrow[...].astype(F32) + xbuf[...].astype(F32)
    xrow2 = rows.astype(BF16)
    l_wq.wait()
    queries = silu(dot(xrow2, wq[...])).astype(BF16)
    qbuf[y, z] = (queries.astype(F32) * (0.5 / math.sqrt(2 * half // HEADS))).astype(BF16)

    def qz_copy(d):
        return remote(qbuf.at[y, z], qbuf.at[y, z], qz_send.at[d - 1], qz_recv.at[d - 1], zpeer(d))

    def qy_copy(d, e):
        block = qbuf.at[y, (z - d + zs) % zs]
        return remote(block, block, qy_send.at[d, e - 1], qy_recv.at[d, e - 1], ypeer(e))

    def qy_relay(d):
        if d > 0:
            qz_copy(d).wait_recv()
        for e in range(1, YS):
            qy_copy(d, e).start()

    for d in range(1, zs):
        qz_copy(d).start()
    qy_relay(0)
    near_relay(0)
    l_wg.wait()
    gates[...] = silu(dot(xrow2, wg[...]))
    qy_relay(1)
    qy_relay(zs - 1)
    near_relay(1)
    for d in (2, zs - 2):
        qy_relay(d)
    far_relay(0)
    for d in range(3, zs - 2):
        qy_relay(d)
    far_relay(1)

    l_m.wait()
    m_copy.wait_recv()
    spot = lax.broadcasted_iota(jnp.int32, (hist, LANES), 0)

    def project(q):
        def block(i, carry):
            b, core = i // CORES, i % CORES
            weights = jnp.concatenate([wbuf[q, 0], wbuf[q, 1]], axis=1)
            raw = dot(mall[core, b], weights)
            at_rows = pl.ds(pl.multiple_of(core * hist, hist), hist)
            kbuf[q, b, at_rows, :] = silu(raw[:, :LANES]).astype(BF16)
            place = (chip * CORES + core) * hist + spot
            vbuf[q, b, at_rows, :] = jnp.where(
                place < ext_ref[b], raw[:, LANES:], 0.0
            ).astype(BF16)
            return carry

        lax.fori_loop(0, 2 * CORES, block, 0)

    def own_chunk(j, carry):
        q = 2 * colour + j

        @pl.when(holds)
        def _():
            wl_copy(q).wait()

        project(q)
        return carry

    lax.fori_loop(0, 2, own_chunk, 0)

    l_wco.wait()
    for b in range(2):
        hidden = dot(cand[b], wco[...])
        pre[b] = silu(hidden[:, :half]) * hidden[:, half:]

    live_row = lax.broadcasted_iota(jnp.int32, (rows16, hist), 0)
    live_col = lax.broadcasted_iota(jnp.int32, (rows16, hist), 1)
    total = jnp.zeros((rows16, half), F32)
    for b in range(2):
        for core in range(CORES):
            place = (chip * CORES + core) * hist + live_col
            mask = jnp.where((live_row == b) & (place < ext_ref[b]), 1.0, 0.0).astype(BF16)
            total = total + dot(mask, mall[core, b, :, lanes(c * half, half)])
    cs[0] = jnp.concatenate(
        [total[:2, i * LANES:(i + 1) * LANES] for i in range(half // LANES)], axis=0
    )

    def cy_copy(d):
        return remote(cs.at[0], csy.at[d - 1], cy_send.at[d - 1], cy_recv.at[d - 1], ypeer(d))

    def cz_copy(d):
        return remote(cs.at[1], csz.at[d - 1], cz_send.at[d - 1], cz_recv.at[d - 1], zpeer(d))

    for d in range(1, YS):
        cy_copy(d).start()

    for j in range(2):
        other = 2 * (1 - colour) + j
        for kv in range(2):
            @pl.when(c + 2 * kv == u)
            def _():
                wl_copy(other).wait()

            @pl.when(c + 2 * kv != u)
            def _():
                for high in range(2):
                    half_ = part(other, kv, high)
                    remote(
                        half_, half_, wf_send.at[j, kv, high], wf_recv.at[j, kv, high], ypeer(1)
                    ).wait_recv()

        project(other)

    for d in range(zs):
        for e in range(1, YS):
            qy_copy(d, e).wait_recv()
    for yy in range(YS):
        block = qbuf[yy].astype(F32)
        for b in range(2):
            own_rows = block[:, b * SLOTS:(b + 1) * SLOTS, :].reshape(zs * SLOTS, half)
            q2[b, yy * zs * SLOTS:(yy + 1) * zs * SLOTS, :] = own_rows.astype(BF16)

    for d in range(1, YS):
        cy_copy(d).wait_recv()
    cs[1] = cs[0] + (csy[0] + csy[1] + csy[2])
    for d in range(1, zs):
        cz_copy(d).start()

    def py_copy(q, d):
        return remote(
            psend.at[q, (y + d) % YS], yrecv.at[q, d - 1],
            py_send.at[q, d - 1], py_recv.at[q, d - 1], ypeer(d),
        )

    def pz_copy(q, d):
        return remote(
            zsend.at[q, (z + d) % zs], zrecv.at[q, d - 1],
            pz_send.at[q, d - 1], pz_recv.at[q, d - 1], zpeer(d),
        )

    lane = lax.broadcasted_iota(jnp.int32, (YS * zs * SLOTS, LANES), 1)
    first = lane < (LANES // 2)

    def compute(q):
        for b in range(2):
            queries_ = q2[b, :, lanes(q * LANES, LANES)]
            outs = []
            for h in range(2):
                keep = first if h == 0 else jnp.logical_not(first)
                masked = jnp.where(keep, queries_.astype(F32), 0.0).astype(BF16)
                logits = dot_nt(masked, kbuf[q, b])
                weights = (logits + logits * jnp.tanh(logits)).astype(BF16)
                outs.append(dot(weights, vbuf[q, b]))
            out = jnp.where(first, outs[0], outs[1])
            pf[:, :, b * SLOTS:(b + 1) * SLOTS, :] = out.reshape(YS, zs, SLOTS, LANES)
        psend[q] = pf[...].astype(BF16)
        pown[q] = pf[y]
        for d in range(1, YS):
            py_copy(q, d).start()

    def reduce_y(q):
        for d in range(1, YS):
            py_copy(q, d).wait_recv()
        total_ = pown[q]
        for d in range(1, YS):
            total_ = total_ + yrecv[q, d - 1].astype(F32)
        pown[q] = total_
        zsend[q] = total_.astype(BF16)
        zown[q] = pown[q, z]
        for d in range(1, zs):
            pz_copy(q, d).start()

    def step(q, carry):
        @pl.when(q < CHUNKS)
        def _():
            compute(q)

        @pl.when(q > 0)
        def _():
            reduce_y(q - 1)

        return carry

    lax.fori_loop(0, CHUNKS + 1, step, 0)

    for d in range(1, zs):
        cz_copy(d).wait_recv()
    packed = cs[1]
    for d in range(1, zs):
        packed = packed + csz[d - 1]
    summed = jnp.concatenate(
        [packed[2 * i:2 * i + 2] for i in range(half // LANES)], axis=1
    )
    summed = jnp.concatenate([summed, jnp.zeros((6, half), F32)], axis=0)
    l_avg.wait()
    part1 = summed.astype(BF16)
    rest = summed - part1.astype(F32)
    part2 = rest.astype(BF16)
    part3 = (rest - part2.astype(F32)).astype(BF16)
    pool[0] = dot(part1, avg[...]) + dot(part2, avg[...]) + dot(part3, avg[...])
    cp_copy = remote(pool.at[0], pool.at[1], cp_sem.at[0], cp_sem.at[1], sibling)
    cp_copy.start()

    def reduce_z(q, carry):
        total_ = zown[q]
        for d in range(1, zs):
            pz_copy(q, d).wait_recv()
            total_ = total_ + zrecv[q, d - 1].astype(F32)
        afull[c, q] = total_
        return carry

    lax.fori_loop(0, CHUNKS, reduce_z, 0)
    a_copy = remote(afull.at[c], afull.at[c], a_sem.at[0], a_sem.at[1], sibling)
    a_copy.start()

    cp_copy.wait_recv()
    pooled = pool[0] + pool[1]
    for b in range(2):
        scale = 1.0 / (
            jnp.sqrt(jnp.full((8, LANES), ext_ref[b], jnp.int32).astype(F32)) * math.sqrt(half)
        )
        scores = lax.dot_general(
            pooled, pre[b], (((1,), (1,)), ((), ())),
            precision=lax.Precision.HIGHEST, preferred_element_type=F32,
        )
        coarse_ref[b:b + 1, :] = (scores * scale)[b:b + 1, :]

    a_copy.wait_recv()
    attention = jnp.concatenate(
        [afull[core, q] for core in range(CORES) for q in range(CHUNKS)], axis=1
    )
    width = 2 * half
    mean = jnp.sum(attention, axis=-1, keepdims=True) * (1.0 / width)
    centred = attention - mean
    variance = jnp.sum(centred * centred, axis=-1, keepdims=True) * (1.0 / width)
    normed = centred / jnp.sqrt(variance + epsilon)
    chosen_rows = xrow[...].astype(F32) + xbuf[...].astype(F32)
    mixed_ref[...] = (normed * gates[...] + chosen_rows).astype(BF16)

    x_copy.wait_send()
    m_copy.wait_send()
    cp_copy.wait_send()
    a_copy.wait_send()

    @pl.when(holds)
    def _():
        for j in range(2):
            for d in (1, 3):
                wx_copy(j, d).wait_send()
            for high in range(2):
                wf_copy(j, 1 - own_kv, high).wait_send()

    @pl.when(jnp.logical_not(holds))
    def _():
        for j in range(2):
            for high in range(2):
                wh_copy(j, 0, high).wait_send()
                for kv in range(2):
                    wf_copy(j, kv, high).wait_send()

    for d in range(1, zs):
        qz_copy(d).wait_send()
        cz_copy(d).wait_send()
    for d in range(1, YS):
        cy_copy(d).wait_send()
    for d in range(zs):
        for e in range(1, YS):
            qy_copy(d, e).wait_send()

    def drain(q, carry):
        for d in range(1, YS):
            py_copy(q, d).wait_send()
        for d in range(1, zs):
            pz_copy(q, d).wait_send()
        return carry

    lax.fori_loop(0, CHUNKS, drain, 0)


def place_kernel(scores_ref, mixed_ref, selt_ref, coarse_ref, fine_ref):
    coarse_ref[...] = scores_ref[...]
    for b in range(fine_ref.shape[0]):
        fine_ref[b] = dot(selt_ref[b], mixed_ref[...]).astype(BF16)


def local(memory, contenders, wc, wm, wco, avg, idx, ext):
    users, hist, width = memory.shape
    entries = contenders.shape[1]
    half = width // 2
    zs = lax.axis_size("seq") // (CORES * YS)
    slots = YS * zs * SLOTS
    dma = pltpu.SemaphoreType.DMA
    vmem = pltpu.VMEM
    any_ = pl.BlockSpec(memory_space=pl.ANY)
    scratch = [
        vmem((users, entries, width), BF16),
        vmem((width, half), BF16),
        vmem((width, width), BF16),
        vmem((width, width), BF16),
        vmem((half, half), BF16),
        vmem((CORES, users, hist, width), BF16),
        vmem((CHUNKS, 2, width, LANES), BF16),
        vmem((2 * SLOTS, width), BF16),
        vmem((2 * SLOTS, width), BF16),
        vmem((2 * SLOTS, width), F32),
        vmem((users, 2 * SLOTS, entries), BF16),
        vmem((YS, zs, 2 * SLOTS, half), BF16),
        vmem((users, slots, half), BF16),
        vmem((CHUNKS, users, CORES * hist, LANES), BF16),
        vmem((CHUNKS, users, CORES * hist, LANES), BF16),
        vmem((YS, zs, 2 * SLOTS, LANES), F32),
        vmem((CHUNKS, YS, zs, 2 * SLOTS, LANES), BF16),
        vmem((CHUNKS, zs, 2 * SLOTS, LANES), F32),
        vmem((CHUNKS, YS - 1, zs, 2 * SLOTS, LANES), BF16),
        vmem((CHUNKS, 2 * SLOTS, LANES), F32),
        vmem((CHUNKS, zs, 2 * SLOTS, LANES), BF16),
        vmem((CHUNKS, zs - 1, 2 * SLOTS, LANES), BF16),
        vmem((CORES, CHUNKS, 2 * SLOTS, LANES), F32),
        vmem((users, entries, half), F32),
        vmem((2, 8, LANES), F32),
        vmem((YS - 1, 8, LANES), F32),
        vmem((zs - 1, 8, LANES), F32),
        vmem((2, 8, half), F32),
        dma((6,)),
        dma((CHUNKS,)),
        dma((2,)),
        dma((2,)),
        dma((2, 2)),
        dma((2, 2)),
        dma((2, 2)),
        dma((2, 2)),
        dma((2, 2, 2)),
        dma((2, 2, 2)),
        dma((zs - 1,)),
        dma((zs - 1,)),
        dma((zs, YS - 1)),
        dma((zs, YS - 1)),
        dma((YS - 1,)),
        dma((YS - 1,)),
        dma((zs - 1,)),
        dma((zs - 1,)),
        dma((2,)),
        dma((CHUNKS, YS - 1)),
        dma((CHUNKS, YS - 1)),
        dma((CHUNKS, zs - 1)),
        dma((CHUNKS, zs - 1)),
        dma((2,)),
    ]
    vm = pl.BlockSpec(memory_space=pltpu.VMEM)
    scores, mixed, selt = pl.pallas_call(
        functools.partial(kernel, zs),
        out_shape=(
            jax.ShapeDtypeStruct((users, entries), F32),
            jax.ShapeDtypeStruct((2 * SLOTS, width), BF16),
            jax.ShapeDtypeStruct((users, entries, 2 * SLOTS), BF16),
        ),
        in_specs=[any_] * 6
        + [pl.BlockSpec(memory_space=pltpu.VMEM), pl.BlockSpec(memory_space=pltpu.SMEM)],
        out_specs=(vm, vm, vm),
        scratch_shapes=scratch,
        compiler_params=pltpu.CompilerParams(
            collective_id=0, has_side_effects=True, vmem_limit_bytes=56 * 1024 * 1024
        ),
        cost_estimate=pl.CostEstimate(
            flops=6_500_000_000, bytes_accessed=12_000_000, transcendentals=7_000_000
        ),
    )(memory, contenders, wc, wm, wco, avg, idx, ext)
    return pl.pallas_call(
        place_kernel,
        out_shape=(
            jax.ShapeDtypeStruct((users, entries), F32),
            jax.ShapeDtypeStruct((users, entries, width), BF16),
        ),
        in_specs=[vm, vm, vm],
        out_specs=(vm, vm),
    )(scores, mixed, selt)


def solution(mesh):
    placed = (
        P("user", "seq", None),
        P("user", "seq", None),
        P(),
        P(None, "user"),
        P(),
        P(),
        P("user", None),
        P("user"),
    )
    return jax.shard_map(
        local,
        mesh=mesh,
        in_specs=placed,
        out_specs=(P("user", "seq"), P("user", "seq", None)),
        check_vma=False,
    )
```

```python
import functools
import math

import jax
import jax.numpy as jnp
from jax import lax
from jax.experimental import pallas as pl
from jax.experimental.pallas import tpu as pltpu
from jax.sharding import PartitionSpec as P

HEADS = 16
CORES = 2
YS = 4
XS = 4
CHUNKS = 4
LANES = 128
SLOTS = 8
epsilon = 1e-05

F32 = jnp.float32
BF16 = jnp.bfloat16
MESH = pl.DeviceIdType.MESH


def dot(a, b):
    return jnp.dot(a, b, preferred_element_type=F32)


def dot_nt(a, b):
    return lax.dot_general(a, b, (((1,), (1,)), ((), ())), preferred_element_type=F32)


def silu(x):
    h = x * 0.5
    return h + h * jnp.tanh(h)


def kernel(
    zs,
    m_hbm, cand_hbm, wc_hbm, wm_hbm, wco_hbm, avg_hbm, idx_ref, ext_ref,
    coarse_ref, mixed_ref, selt,
    cand, wq, wg, wco, avg, mall, wbuf,
    xbuf, xrow, gates, sel,
    qbuf, q2, kbuf, vbuf, pf, psend, pown, yrecv, zown, zsend, zrecv, afull,
    pre, cs, csy, csz, pool,
    local_sem, wl_sem, m_sem, x_sem, wx_send, wx_recv, wh_send, wh_recv, wf_send, wf_recv,
    qz_send, qz_recv, qy_send, qy_recv,
    cy_send, cy_recv, cz_send, cz_recv, cp_sem,
    py_send, py_recv, pz_send, pz_recv, a_sem, far_sem,
):
    u = lax.axis_index("user")
    s = lax.axis_index("seq")
    c = s % CORES
    y = (s // CORES) % YS
    z = s // (CORES * YS)
    chip = s // CORES
    hist = m_hbm.shape[1]
    half = wq.shape[1]
    colour = (y + z) % 2

    def at(x_, z_, y_, c_):
        return (x_, (z_ * YS + y_) * CORES + c_)

    sibling = at(u, z, y, 1 - c)

    def xpeer(d):
        return at((u + d) % XS, z, y, c)

    def ypeer(d):
        return at(u, z, (y + d) % YS, c)

    def zpeer(d):
        return at(u, (z + d) % zs, y, c)

    def lanes(start, size):
        return pl.ds(pl.multiple_of(start, LANES), size)

    def remote(src, dst, send, recv, device):
        return pltpu.make_async_remote_copy(
            src_ref=src, dst_ref=dst, send_sem=send, recv_sem=recv,
            device_id=device, device_id_type=MESH,
        )

    l_cand = pltpu.make_async_copy(cand_hbm, cand, local_sem.at[0])
    l_wq = pltpu.make_async_copy(
        wc_hbm.at[:, lanes(2 * half + c * half, half)], wq, local_sem.at[1]
    )
    l_m = pltpu.make_async_copy(m_hbm, mall.at[:, c], local_sem.at[2])
    l_wg = pltpu.make_async_copy(wc_hbm.at[:, pl.ds(0, 2 * half)], wg, local_sem.at[3])
    l_wco = pltpu.make_async_copy(wco_hbm, wco, local_sem.at[4])
    l_avg = pltpu.make_async_copy(
        avg_hbm.at[pl.ds(pl.multiple_of(c * half, half), half), :], avg, local_sem.at[5]
    )
    l_cand.start()
    l_wq.start()

    own_kv = u // 2
    holds = (u % 2) == c

    def wl_copy(q):
        return pltpu.make_async_copy(
            wm_hbm.at[:, lanes(q * LANES, LANES)], wbuf.at[q, own_kv], wl_sem.at[q]
        )

    @pl.when(holds)
    def _():
        for i in range(CHUNKS):
            wl_copy((2 * colour + i) % CHUNKS).start()

    barrier = pltpu.get_barrier_semaphore()

    def greet(device):
        pl.semaphore_signal(barrier, inc=1, device_id=device, device_id_type=MESH)

    greet(sibling)
    for peer, size in ((xpeer, XS), (ypeer, YS), (zpeer, zs)):
        greet(peer(1))
        greet(peer(size - 1))

    l_m.start()
    l_wg.start()
    l_wco.start()
    l_avg.start()

    rows16 = 2 * SLOTS
    ones = jnp.ones((rows16, idx_ref.shape[1]), BF16)
    pair = 2 * cand_hbm.shape[1]
    mine = cand_hbm.shape[1]
    upper = jnp.where(
        lax.broadcasted_iota(jnp.int32, (pair, pair), 0)
        < lax.broadcasted_iota(jnp.int32, (pair, pair), 1),
        1.0, 0.0,
    ).astype(BF16)
    eye = jnp.where(
        lax.broadcasted_iota(jnp.int32, (mine, mine), 0)
        == lax.broadcasted_iota(jnp.int32, (mine, mine), 1),
        1.0, 0.0,
    ).astype(BF16)
    row = lax.broadcasted_iota(jnp.int32, (rows16, pair), 0)
    for b in range(2):
        near = idx_ref[b:b + 1, :] - chip * pair
        matches = jnp.where(
            lax.broadcasted_iota(jnp.int32, (pair, idx_ref.shape[1]), 0) == near, 1.0, 0.0
        ).astype(BF16)
        flagged = dot_nt(ones, matches)
        placing = dot(flagged.astype(BF16), upper)
        target = (row - b * SLOTS).astype(F32)
        chosen = jnp.where((flagged > 0.5) & (jnp.abs(placing - target) < 0.5), 1.0, 0.0)
        chosen = jnp.where((row // SLOTS) == b, chosen, 0.0)
        own = jnp.where(c == 0, chosen[:, :mine], chosen[:, mine:]).astype(BF16)
        sel[b] = own
        selt[b] = dot_nt(eye, own).astype(BF16)

    l_cand.wait()
    found = dot(sel[0], cand[0]) + dot(sel[1], cand[1])
    xrow[...] = found.astype(BF16)

    pl.semaphore_wait(barrier, 7)

    def tell(r, peer, size):
        for side, d in ((0, 1), (1, size - 1)):
            pl.semaphore_signal(
                far_sem.at[r, side], inc=1, device_id=peer(d), device_id_type=MESH
            )

    def hear(r):
        for side in range(2):
            pl.semaphore_wait(far_sem.at[r, side], 1)

    rounds = zs // 2 - 1
    tell(0, zpeer, zs)
    tell(rounds, ypeer, YS)

    x_copy = remote(xrow, xbuf, x_sem.at[0], x_sem.at[1], sibling)
    x_copy.start()

    m_copy = remote(m_hbm, mall.at[:, c], m_sem.at[0], m_sem.at[1], sibling)
    m_copy.start()

    depth = wbuf.shape[2] // 2

    def part(q, kv, high):
        return wbuf.at[q, kv, pl.ds(pl.multiple_of(high * depth, depth), depth)]

    def wx_copy(j, high, d):
        half_ = part(2 * colour + j, own_kv, high)
        return remote(
            half_, half_, wx_send.at[j, high, d // 2], wx_recv.at[j, high, own_kv], xpeer(d)
        )

    @pl.when(holds)
    def _():
        for i in range(2):
            for j in range(2):
                if i == 0:
                    wl_copy(2 * colour + j).wait()
                wx_copy(j, i, 1).start()
                wx_copy(j, 1 - i, XS - 1).start()

    def wh_copy(j, kv, high):
        half_ = part(2 * colour + j, kv, high)
        return remote(
            half_, half_, wh_send.at[j, high], wh_recv.at[j, high],
            xpeer(1 + high * (XS - 2)),
        )

    def wf_copy(j, kv, high):
        half_ = part(2 * colour + j, kv, high)
        if j == 0:
            device = ypeer(1 + high * (YS - 2))
        else:
            device = zpeer(1 + high * (zs - 2))
        return remote(
            half_, half_, wf_send.at[j, kv, high], wf_recv.at[j, kv, high], device
        )

    def near_relay(i, j):
        @pl.when(jnp.logical_not(holds))
        def _():
            for kv in range(2):
                behind = (c + 2 * kv + 1) % XS == u
                high = jnp.where(behind, i, 1 - i)
                half_ = part(2 * colour + j, kv, high)
                remote(
                    half_, half_, wx_send.at[j, high, 0], wx_recv.at[j, high, kv], xpeer(1)
                ).wait_recv()
                if i == 0:
                    wh_copy(j, kv, high).start()
                wf_copy(j, kv, high).start()

    def far_relay(j):
        @pl.when(holds)
        def _():
            for high in range(2):
                half_ = part(2 * colour + j, 1 - own_kv, high)
                remote(
                    half_, half_, wh_send.at[j, high], wh_recv.at[j, high], xpeer(1)
                ).wait_recv()
                wf_copy(j, 1 - own_kv, high).start()

    x_copy.wait_recv()
    rows = xrow[...].astype(F32) + xbuf[...].astype(F32)
    xrow2 = rows.astype(BF16)
    hear(0)
    tell(1, zpeer, zs)
    l_wq.wait()
    queries = silu(dot(xrow2, wq[...])).astype(BF16)
    qbuf[y, z] = (queries.astype(F32) * (0.5 / math.sqrt(2 * half // HEADS))).astype(BF16)

    def qz_copy(d):
        return remote(qbuf.at[y, z], qbuf.at[y, z], qz_send.at[d - 1], qz_recv.at[d - 1], zpeer(d))

    def qy_copy(d, e):
        block = qbuf.at[y, (z - d + zs) % zs]
        return remote(block, block, qy_send.at[d, e - 1], qy_recv.at[d, e - 1], ypeer(e))

    def qy_relay(d):
        if d > 0:
            qz_copy(d).wait_recv()
        for e in range(1, YS):
            qy_copy(d, e).start()

    for d in (1, zs - 1, 2, zs - 2):
        qz_copy(d).start()
    near_relay(0, 0)
    for r in range(1, rounds):
        hear(r)
        if r + 1 < rounds:
            tell(r + 1, zpeer, zs)
        for d in sorted({r + 2, zs - r - 2}):
            qz_copy(d).start()
    hear(rounds)
    qy_relay(0)
    near_relay(0, 1)
    l_wg.wait()
    gates[...] = silu(dot(xrow2, wg[...]))
    qy_relay(1)
    qy_relay(zs - 1)
    near_relay(1, 0)
    far_relay(0)
    near_relay(1, 1)
    for d in (2, zs - 2):
        qy_relay(d)
    far_relay(1)
    for d in range(3, zs - 2):
        qy_relay(d)

    l_m.wait()
    m_copy.wait_recv()
    both = CORES * hist
    spot = chip * both + lax.broadcasted_iota(jnp.int32, (both, LANES), 0)

    def project(q):
        def block(b, carry):
            weights = jnp.concatenate([wbuf[q, 0], wbuf[q, 1]], axis=1)
            raw = dot(mall[b].reshape(both, 2 * half), weights)
            kbuf[q, b] = silu(raw[:, :LANES]).astype(BF16)
            vbuf[q, b] = jnp.where(spot < ext_ref[b], raw[:, LANES:], 0.0).astype(BF16)
            return carry

        lax.fori_loop(0, 2, block, 0)

    def own_chunk(j, carry):
        project(2 * colour + j)
        return carry

    lax.fori_loop(0, 2, own_chunk, 0)

    l_wco.wait()
    for b in range(2):
        hidden = dot(cand[b], wco[...])
        pre[b] = silu(hidden[:, :half]) * hidden[:, half:]

    live_row = lax.broadcasted_iota(jnp.int32, (rows16, hist), 0)
    live_col = lax.broadcasted_iota(jnp.int32, (rows16, hist), 1)
    total = jnp.zeros((rows16, half), F32)
    for b in range(2):
        for core in range(CORES):
            place = (chip * CORES + core) * hist + live_col
            mask = jnp.where((live_row == b) & (place < ext_ref[b]), 1.0, 0.0).astype(BF16)
            total = total + dot(mask, mall[b, core, :, lanes(c * half, half)])
    cs[0] = jnp.concatenate(
        [total[:2, i * LANES:(i + 1) * LANES] for i in range(half // LANES)], axis=0
    )

    def cy_copy(d):
        return remote(cs.at[0], csy.at[d - 1], cy_send.at[d - 1], cy_recv.at[d - 1], ypeer(d))

    def cz_copy(d):
        return remote(cs.at[1], csz.at[d - 1], cz_send.at[d - 1], cz_recv.at[d - 1], zpeer(d))

    for d in range(1, YS):
        cy_copy(d).start()

    for j in range(2):
        other = 2 * (1 - colour) + j
        for kv in range(2):
            @pl.when(c + 2 * kv == u)
            def _():
                wl_copy(other).wait()

            @pl.when(c + 2 * kv != u)
            def _():
                for high in range(2):
                    half_ = part(other, kv, high)
                    remote(
                        half_, half_, wf_send.at[j, kv, high], wf_recv.at[j, kv, high], ypeer(1)
                    ).wait_recv()

        project(other)

    for d in range(zs):
        for e in range(1, YS):
            qy_copy(d, e).wait_recv()
    for yy in range(YS):
        block = qbuf[yy].astype(F32)
        for b in range(2):
            own_rows = block[:, b * SLOTS:(b + 1) * SLOTS, :].reshape(zs * SLOTS, half)
            q2[b, yy * zs * SLOTS:(yy + 1) * zs * SLOTS, :] = own_rows.astype(BF16)

    for d in range(1, YS):
        cy_copy(d).wait_recv()
    cs[1] = cs[0] + (csy[0] + csy[1] + csy[2])
    for d in range(1, zs):
        cz_copy(d).start()

    def py_copy(q, d):
        return remote(
            psend.at[q, (y + d) % YS], yrecv.at[q, d - 1],
            py_send.at[q, d - 1], py_recv.at[q, d - 1], ypeer(d),
        )

    def pz_copy(q, d):
        return remote(
            zsend.at[q, (z + d) % zs], zrecv.at[q, d - 1],
            pz_send.at[q, d - 1], pz_recv.at[q, d - 1], zpeer(d),
        )

    lane = lax.broadcasted_iota(jnp.int32, (YS * zs * SLOTS, LANES), 1)
    first = lane < (LANES // 2)

    def compute(q):
        for b in range(2):
            queries_ = q2[b, :, lanes(q * LANES, LANES)]
            outs = []
            for h in range(2):
                keep = first if h == 0 else jnp.logical_not(first)
                masked = jnp.where(keep, queries_.astype(F32), 0.0).astype(BF16)
                logits = dot_nt(masked, kbuf[q, b])
                weights = (logits + logits * jnp.tanh(logits)).astype(BF16)
                outs.append(dot(weights, vbuf[q, b]))
            out = jnp.where(first, outs[0], outs[1])
            pf[:, :, b * SLOTS:(b + 1) * SLOTS, :] = out.reshape(YS, zs, SLOTS, LANES)
        psend[q] = pf[...].astype(BF16)
        pown[q] = pf[y]
        for d in range(1, YS):
            py_copy(q, d).start()

    def reduce_y(q):
        for d in range(1, YS):
            py_copy(q, d).wait_recv()
        total_ = pown[q]
        for d in range(1, YS):
            total_ = total_ + yrecv[q, d - 1].astype(F32)
        pown[q] = total_
        zsend[q] = total_.astype(BF16)
        zown[q] = pown[q, z]
        for d in range(1, zs):
            pz_copy(q, d).start()

    def step(q, carry):
        @pl.when(q < CHUNKS)
        def _():
            compute(q)

        @pl.when(q > 0)
        def _():
            reduce_y(q - 1)

        return carry

    lax.fori_loop(0, CHUNKS + 1, step, 0)

    for d in range(1, zs):
        cz_copy(d).wait_recv()
    packed = cs[1]
    for d in range(1, zs):
        packed = packed + csz[d - 1]
    summed = jnp.concatenate(
        [packed[2 * i:2 * i + 2] for i in range(half // LANES)], axis=1
    )
    summed = jnp.concatenate([summed, jnp.zeros((6, half), F32)], axis=0)
    l_avg.wait()
    part1 = summed.astype(BF16)
    rest = summed - part1.astype(F32)
    part2 = rest.astype(BF16)
    part3 = (rest - part2.astype(F32)).astype(BF16)
    pool[0] = dot(part1, avg[...]) + dot(part2, avg[...]) + dot(part3, avg[...])
    cp_copy = remote(pool.at[0], pool.at[1], cp_sem.at[0], cp_sem.at[1], sibling)
    cp_copy.start()

    def reduce_z(q, carry):
        total_ = zown[q]
        for d in range(1, zs):
            pz_copy(q, d).wait_recv()
            total_ = total_ + zrecv[q, d - 1].astype(F32)
        afull[c, q] = total_
        return carry

    lax.fori_loop(0, CHUNKS, reduce_z, 0)
    a_copy = remote(afull.at[c], afull.at[c], a_sem.at[0], a_sem.at[1], sibling)
    a_copy.start()

    cp_copy.wait_recv()
    pooled = pool[0] + pool[1]
    for b in range(2):
        scale = 1.0 / (
            jnp.sqrt(jnp.full((8, LANES), ext_ref[b], jnp.int32).astype(F32)) * math.sqrt(half)
        )
        scores = lax.dot_general(
            pooled, pre[b], (((1,), (1,)), ((), ())),
            precision=lax.Precision.HIGHEST, preferred_element_type=F32,
        )
        coarse_ref[b:b + 1, :] = (scores * scale)[b:b + 1, :]

    a_copy.wait_recv()
    attention = jnp.concatenate(
        [afull[core, q] for core in range(CORES) for q in range(CHUNKS)], axis=1
    )
    width = 2 * half
    mean = jnp.sum(attention, axis=-1, keepdims=True) * (1.0 / width)
    centred = attention - mean
    variance = jnp.sum(centred * centred, axis=-1, keepdims=True) * (1.0 / width)
    normed = centred / jnp.sqrt(variance + epsilon)
    chosen_rows = xrow[...].astype(F32) + xbuf[...].astype(F32)
    mixed_ref[...] = (normed * gates[...] + chosen_rows).astype(BF16)

    x_copy.wait_send()
    m_copy.wait_send()
    cp_copy.wait_send()
    a_copy.wait_send()

    @pl.when(holds)
    def _():
        for j in range(2):
            for high in range(2):
                wx_copy(j, high, 1).wait_send()
                wx_copy(j, high, XS - 1).wait_send()
                wf_copy(j, 1 - own_kv, high).wait_send()

    @pl.when(jnp.logical_not(holds))
    def _():
        for j in range(2):
            for high in range(2):
                wh_copy(j, 0, high).wait_send()
                for kv in range(2):
                    wf_copy(j, kv, high).wait_send()

    for d in range(1, zs):
        qz_copy(d).wait_send()
        cz_copy(d).wait_send()
    for d in range(1, YS):
        cy_copy(d).wait_send()
    for d in range(zs):
        for e in range(1, YS):
            qy_copy(d, e).wait_send()

    def drain(q, carry):
        for d in range(1, YS):
            py_copy(q, d).wait_send()
        for d in range(1, zs):
            pz_copy(q, d).wait_send()
        return carry

    lax.fori_loop(0, CHUNKS, drain, 0)


def place_kernel(scores_ref, mixed_ref, selt_ref, coarse_ref, fine_ref):
    coarse_ref[...] = scores_ref[...]
    for b in range(fine_ref.shape[0]):
        fine_ref[b] = dot(selt_ref[b], mixed_ref[...]).astype(BF16)


def local(memory, contenders, wc, wm, wco, avg, idx, ext):
    users, hist, width = memory.shape
    entries = contenders.shape[1]
    half = width // 2
    zs = lax.axis_size("seq") // (CORES * YS)
    slots = YS * zs * SLOTS
    dma = pltpu.SemaphoreType.DMA
    vmem = pltpu.VMEM
    any_ = pl.BlockSpec(memory_space=pl.ANY)
    scratch = [
        vmem((users, entries, width), BF16),
        vmem((width, half), BF16),
        vmem((width, width), BF16),
        vmem((width, width), BF16),
        vmem((half, half), BF16),
        vmem((users, CORES, hist, width), BF16),
        vmem((CHUNKS, 2, width, LANES), BF16),
        vmem((2 * SLOTS, width), BF16),
        vmem((2 * SLOTS, width), BF16),
        vmem((2 * SLOTS, width), F32),
        vmem((users, 2 * SLOTS, entries), BF16),
        vmem((YS, zs, 2 * SLOTS, half), BF16),
        vmem((users, slots, half), BF16),
        vmem((CHUNKS, users, CORES * hist, LANES), BF16),
        vmem((CHUNKS, users, CORES * hist, LANES), BF16),
        vmem((YS, zs, 2 * SLOTS, LANES), F32),
        vmem((CHUNKS, YS, zs, 2 * SLOTS, LANES), BF16),
        vmem((CHUNKS, zs, 2 * SLOTS, LANES), F32),
        vmem((CHUNKS, YS - 1, zs, 2 * SLOTS, LANES), BF16),
        vmem((CHUNKS, 2 * SLOTS, LANES), F32),
        vmem((CHUNKS, zs, 2 * SLOTS, LANES), BF16),
        vmem((CHUNKS, zs - 1, 2 * SLOTS, LANES), BF16),
        vmem((CORES, CHUNKS, 2 * SLOTS, LANES), F32),
        vmem((users, entries, half), F32),
        vmem((2, 8, LANES), F32),
        vmem((YS - 1, 8, LANES), F32),
        vmem((zs - 1, 8, LANES), F32),
        vmem((2, 8, half), F32),
        dma((6,)),
        dma((CHUNKS,)),
        dma((2,)),
        dma((2,)),
        dma((2, 2, 2)),
        dma((2, 2, 2)),
        dma((2, 2)),
        dma((2, 2)),
        dma((2, 2, 2)),
        dma((2, 2, 2)),
        dma((zs - 1,)),
        dma((zs - 1,)),
        dma((zs, YS - 1)),
        dma((zs, YS - 1)),
        dma((YS - 1,)),
        dma((YS - 1,)),
        dma((zs - 1,)),
        dma((zs - 1,)),
        dma((2,)),
        dma((CHUNKS, YS - 1)),
        dma((CHUNKS, YS - 1)),
        dma((CHUNKS, zs - 1)),
        dma((CHUNKS, zs - 1)),
        dma((2,)),
        pltpu.SemaphoreType.REGULAR((zs // 2, 2)),
    ]
    vm = pl.BlockSpec(memory_space=pltpu.VMEM)
    scores, mixed, selt = pl.pallas_call(
        functools.partial(kernel, zs),
        out_shape=(
            jax.ShapeDtypeStruct((users, entries), F32),
            jax.ShapeDtypeStruct((2 * SLOTS, width), BF16),
            jax.ShapeDtypeStruct((users, entries, 2 * SLOTS), BF16),
        ),
        in_specs=[any_] * 6
        + [pl.BlockSpec(memory_space=pltpu.VMEM), pl.BlockSpec(memory_space=pltpu.SMEM)],
        out_specs=(vm, vm, vm),
        scratch_shapes=scratch,
        compiler_params=pltpu.CompilerParams(
            collective_id=0, has_side_effects=True, vmem_limit_bytes=56 * 1024 * 1024
        ),
        cost_estimate=pl.CostEstimate(
            flops=6_500_000_000, bytes_accessed=12_000_000, transcendentals=7_000_000
        ),
    )(memory, contenders, wc, wm, wco, avg, idx, ext)
    return pl.pallas_call(
        place_kernel,
        out_shape=(
            jax.ShapeDtypeStruct((users, entries), F32),
            jax.ShapeDtypeStruct((users, entries, width), BF16),
        ),
        in_specs=[vm, vm, vm],
        out_specs=(vm, vm),
    )(scores, mixed, selt)


def solution(mesh):
    placed = (
        P("user", "seq", None),
        P("user", "seq", None),
        P(),
        P(None, "user"),
        P(),
        P(),
        P("user", None),
        P("user"),
    )
    return jax.shard_map(
        local,
        mesh=mesh,
        in_specs=placed,
        out_specs=(P("user", "seq"), P("user", "seq", None)),
        check_vma=False,
    )
```

```python
import functools
import math

import jax
import jax.numpy as jnp
from jax import lax
from jax.experimental import pallas as pl
from jax.experimental.pallas import tpu as pltpu
from jax.sharding import PartitionSpec as P

HEADS = 16
CORES = 2
YS = 4
XS = 4
CHUNKS = 4
LANES = 128
SLOTS = 8
epsilon = 1e-05

F32 = jnp.float32
BF16 = jnp.bfloat16
MESH = pl.DeviceIdType.MESH


def dot(a, b):
    return jnp.dot(a, b, preferred_element_type=F32)


def dot_nt(a, b):
    return lax.dot_general(a, b, (((1,), (1,)), ((), ())), preferred_element_type=F32)


def silu(x):
    h = x * 0.5
    return h + h * jnp.tanh(h)


def kernel(
    zs,
    m_hbm, cand_hbm, wc_hbm, wm_hbm, wco_hbm, avg_hbm, idx_ref, ext_ref,
    coarse_ref, mixed_ref, selt,
    cand, wq, wg, wco, avg, mall, wbuf,
    xbuf, xrow, gates, sel,
    qbuf, q2, kbuf, vbuf, pf, psend, pown, yrecv, zown, zsend, zrecv, afull,
    pre, cs, csy, csz, pool,
    local_sem, wl_sem, m_sem, x_sem, wx_send, wx_recv, wh_send, wh_recv, wf_send, wf_recv,
    qz_send, qz_recv, qy_send, qy_recv,
    cy_send, cy_recv, cz_send, cz_recv, cp_sem,
    py_send, py_recv, pz_send, pz_recv, a_sem, far_sem,
):
    u = lax.axis_index("user")
    s = lax.axis_index("seq")
    c = s % CORES
    y = (s // CORES) % YS
    z = s // (CORES * YS)
    chip = s // CORES
    hist = m_hbm.shape[1]
    half = wq.shape[1]
    colour = (y + z) % 2

    def at(x_, z_, y_, c_):
        return (x_, (z_ * YS + y_) * CORES + c_)

    sibling = at(u, z, y, 1 - c)

    def xpeer(d):
        return at((u + d) % XS, z, y, c)

    def ypeer(d):
        return at(u, z, (y + d) % YS, c)

    def zpeer(d):
        return at(u, (z + d) % zs, y, c)

    def lanes(start, size):
        return pl.ds(pl.multiple_of(start, LANES), size)

    def remote(src, dst, send, recv, device):
        return pltpu.make_async_remote_copy(
            src_ref=src, dst_ref=dst, send_sem=send, recv_sem=recv,
            device_id=device, device_id_type=MESH,
        )

    def settle(ref, sem):
        pltpu.make_async_copy(ref, ref, sem).wait()

    l_cand = pltpu.make_async_copy(cand_hbm, cand, local_sem.at[0])
    l_wq = pltpu.make_async_copy(
        wc_hbm.at[:, lanes(2 * half + c * half, half)], wq, local_sem.at[1]
    )
    l_m = pltpu.make_async_copy(m_hbm, mall.at[:, c], local_sem.at[2])
    l_wg = pltpu.make_async_copy(wc_hbm.at[:, pl.ds(0, 2 * half)], wg, local_sem.at[3])
    l_wco = pltpu.make_async_copy(wco_hbm, wco, local_sem.at[4])
    l_avg = pltpu.make_async_copy(
        avg_hbm.at[pl.ds(pl.multiple_of(c * half, half), half), :], avg, local_sem.at[5]
    )
    l_cand.start()
    l_wq.start()

    own_kv = u // 2
    holds = (u % 2) == c

    def wl_copy(q):
        return pltpu.make_async_copy(
            wm_hbm.at[:, lanes(q * LANES, LANES)], wbuf.at[q, own_kv], wl_sem.at[q]
        )

    @pl.when(holds)
    def _():
        for i in range(CHUNKS):
            wl_copy((2 * colour + i) % CHUNKS).start()

    barrier = pltpu.get_barrier_semaphore()

    def greet(device):
        pl.semaphore_signal(barrier, inc=1, device_id=device, device_id_type=MESH)

    greet(sibling)
    for peer, size in ((xpeer, XS), (ypeer, YS), (zpeer, zs)):
        greet(peer(1))
        greet(peer(size - 1))

    l_m.start()
    l_wg.start()
    l_wco.start()
    l_avg.start()

    rows16 = 2 * SLOTS
    ones = jnp.ones((rows16, idx_ref.shape[1]), BF16)
    pair = 2 * cand_hbm.shape[1]
    mine = cand_hbm.shape[1]
    upper = jnp.where(
        lax.broadcasted_iota(jnp.int32, (pair, pair), 0)
        < lax.broadcasted_iota(jnp.int32, (pair, pair), 1),
        1.0, 0.0,
    ).astype(BF16)
    eye = jnp.where(
        lax.broadcasted_iota(jnp.int32, (mine, mine), 0)
        == lax.broadcasted_iota(jnp.int32, (mine, mine), 1),
        1.0, 0.0,
    ).astype(BF16)
    row = lax.broadcasted_iota(jnp.int32, (rows16, pair), 0)
    for b in range(2):
        near = idx_ref[b:b + 1, :] - chip * pair
        matches = jnp.where(
            lax.broadcasted_iota(jnp.int32, (pair, idx_ref.shape[1]), 0) == near, 1.0, 0.0
        ).astype(BF16)
        flagged = dot_nt(ones, matches)
        placing = dot(flagged.astype(BF16), upper)
        target = (row - b * SLOTS).astype(F32)
        chosen = jnp.where((flagged > 0.5) & (jnp.abs(placing - target) < 0.5), 1.0, 0.0)
        chosen = jnp.where((row // SLOTS) == b, chosen, 0.0)
        own = jnp.where(c == 0, chosen[:, :mine], chosen[:, mine:]).astype(BF16)
        sel[b] = own
        selt[b] = dot_nt(eye, own).astype(BF16)

    l_cand.wait()
    found = dot(sel[0], cand[0]) + dot(sel[1], cand[1])
    xrow[...] = found.astype(BF16)

    pl.semaphore_wait(barrier, 7)

    def tell(r, peer, size):
        for side, d in ((0, 1), (1, size - 1)):
            pl.semaphore_signal(
                far_sem.at[r, side], inc=1, device_id=peer(d), device_id_type=MESH
            )

    def hear(r):
        for side in range(2):
            pl.semaphore_wait(far_sem.at[r, side], 1)

    rounds = zs // 2 - 1
    tell(0, zpeer, zs)
    tell(rounds, ypeer, YS)

    x_copy = remote(xrow, xbuf, x_sem.at[0], x_sem.at[1], sibling)
    x_copy.start()

    m_copy = remote(m_hbm, mall.at[:, c], m_sem.at[0], m_sem.at[1], sibling)
    m_copy.start()

    depth = wbuf.shape[2] // 2

    def part(q, kv, high):
        return wbuf.at[q, kv, pl.ds(pl.multiple_of(high * depth, depth), depth)]

    def wx_copy(j, high, d):
        half_ = part(2 * colour + j, own_kv, high)
        return remote(
            half_, half_, wx_send.at[j, high, d // 2], wx_recv.at[j, high, own_kv], xpeer(d)
        )

    @pl.when(holds)
    def _():
        for i in range(2):
            for j in range(2):
                if i == 0:
                    wl_copy(2 * colour + j).wait()
                wx_copy(j, i, 1).start()
                wx_copy(j, 1 - i, XS - 1).start()

    def wh_copy(j, kv, high):
        half_ = part(2 * colour + j, kv, high)
        return remote(
            half_, half_, wh_send.at[j, high], wh_recv.at[j, high],
            xpeer(1 + high * (XS - 2)),
        )

    def wf_copy(j, kv, high):
        half_ = part(2 * colour + j, kv, high)
        if j == 0:
            device = ypeer(1 + high * (YS - 2))
        else:
            device = zpeer(1 + high * (zs - 2))
        return remote(
            half_, half_, wf_send.at[j, kv, high], wf_recv.at[j, kv, high], device
        )

    def near_relay(i, j):
        @pl.when(jnp.logical_not(holds))
        def _():
            for kv in range(2):
                behind = (c + 2 * kv + 1) % XS == u
                high = jnp.where(behind, i, 1 - i)
                half_ = part(2 * colour + j, kv, high)
                remote(
                    half_, half_, wx_send.at[j, high, 0], wx_recv.at[j, high, kv], xpeer(1)
                ).wait_recv()
                if i == 0:
                    wh_copy(j, kv, high).start()
                wf_copy(j, kv, high).start()

    def far_relay(j):
        @pl.when(holds)
        def _():
            for high in range(2):
                half_ = part(2 * colour + j, 1 - own_kv, high)
                remote(
                    half_, half_, wh_send.at[j, high], wh_recv.at[j, high], xpeer(1)
                ).wait_recv()
                wf_copy(j, 1 - own_kv, high).start()

    x_copy.wait_recv()
    rows = xrow[...].astype(F32) + xbuf[...].astype(F32)
    xrow2 = rows.astype(BF16)
    hear(0)
    tell(1, zpeer, zs)
    l_wq.wait()
    queries = silu(dot(xrow2, wq[...])).astype(BF16)
    qbuf[y, z] = (queries.astype(F32) * (0.5 / math.sqrt(2 * half // HEADS))).astype(BF16)

    def qz_copy(d):
        return remote(qbuf.at[y, z], qbuf.at[y, z], qz_send.at[d - 1], qz_recv.at[d - 1], zpeer(d))

    def qy_copy(d, e):
        block = qbuf.at[y, (z - d + zs) % zs]
        return remote(block, block, qy_send.at[0], qy_recv.at[0], ypeer(e))

    def qy_relay(d):
        if d > 0:
            qz_copy(d).wait_recv()
        for e in range(1, YS):
            qy_copy(d, e).start()

    for d in (1, zs - 1, 2, zs - 2):
        qz_copy(d).start()
    near_relay(0, 0)
    for r in range(1, rounds):
        hear(r)
        if r + 1 < rounds:
            tell(r + 1, zpeer, zs)
        for d in sorted({r + 2, zs - r - 2}):
            qz_copy(d).start()
    hear(rounds)
    qy_relay(0)
    near_relay(0, 1)
    l_wg.wait()
    gates[...] = silu(dot(xrow2, wg[...]))
    qy_relay(1)
    qy_relay(zs - 1)
    near_relay(1, 0)
    far_relay(0)
    near_relay(1, 1)
    for d in (2, zs - 2):
        qy_relay(d)
    far_relay(1)
    for d in range(3, zs - 2):
        qy_relay(d)

    l_m.wait()
    m_copy.wait_recv()
    both = CORES * hist
    spot = chip * both + lax.broadcasted_iota(jnp.int32, (both, LANES), 0)

    def project(q):
        def block(b, carry):
            weights = jnp.concatenate([wbuf[q, 0], wbuf[q, 1]], axis=1)
            raw = dot(mall[b].reshape(both, 2 * half), weights)
            kbuf[q, b] = silu(raw[:, :LANES]).astype(BF16)
            vbuf[q, b] = jnp.where(spot < ext_ref[b], raw[:, LANES:], 0.0).astype(BF16)
            return carry

        lax.fori_loop(0, 2, block, 0)

    def own_chunk(j, carry):
        project(2 * colour + j)
        return carry

    lax.fori_loop(0, 2, own_chunk, 0)

    l_wco.wait()
    for b in range(2):
        hidden = dot(cand[b], wco[...])
        pre[b] = silu(hidden[:, :half]) * hidden[:, half:]

    live_row = lax.broadcasted_iota(jnp.int32, (rows16, hist), 0)
    live_col = lax.broadcasted_iota(jnp.int32, (rows16, hist), 1)
    total = jnp.zeros((rows16, half), F32)
    for b in range(2):
        for core in range(CORES):
            place = (chip * CORES + core) * hist + live_col
            mask = jnp.where((live_row == b) & (place < ext_ref[b]), 1.0, 0.0).astype(BF16)
            total = total + dot(mask, mall[b, core, :, lanes(c * half, half)])
    cs[0] = jnp.concatenate(
        [total[:2, i * LANES:(i + 1) * LANES] for i in range(half // LANES)], axis=0
    )

    def cy_copy(d):
        return remote(cs.at[0], csy.at[d - 1], cy_send.at[0], cy_recv.at[0], ypeer(d))

    def cz_copy(d):
        return remote(cs.at[1], csz.at[d - 1], cz_send.at[0], cz_recv.at[0], zpeer(d))

    for d in range(1, YS):
        cy_copy(d).start()

    for j in range(2):
        other = 2 * (1 - colour) + j
        for kv in range(2):
            @pl.when(c + 2 * kv == u)
            def _():
                wl_copy(other).wait()

            @pl.when(c + 2 * kv != u)
            def _():
                for high in range(2):
                    half_ = part(other, kv, high)
                    remote(
                        half_, half_, wf_send.at[j, kv, high], wf_recv.at[j, kv, high], ypeer(1)
                    ).wait_recv()

        project(other)

    others = qbuf.at[pl.ds(0, YS - 1)]
    settle(others, qy_recv.at[0])
    for yy in range(YS):
        block = qbuf[yy].astype(F32)
        for b in range(2):
            own_rows = block[:, b * SLOTS:(b + 1) * SLOTS, :].reshape(zs * SLOTS, half)
            q2[b, yy * zs * SLOTS:(yy + 1) * zs * SLOTS, :] = own_rows.astype(BF16)

    settle(csy, cy_recv.at[0])
    cs[1] = cs[0] + (csy[0] + csy[1] + csy[2])
    for d in range(1, zs):
        cz_copy(d).start()

    def py_copy(q, d):
        return remote(
            psend.at[q, (y + d) % YS], yrecv.at[q, d - 1],
            py_send.at[q], py_recv.at[q], ypeer(d),
        )

    def pz_copy(q, d):
        return remote(
            zsend.at[q, (z + d) % zs], zrecv.at[q, d - 1],
            pz_send.at[q], pz_recv.at[q], zpeer(d),
        )

    lane = lax.broadcasted_iota(jnp.int32, (YS * zs * SLOTS, LANES), 1)
    first = lane < (LANES // 2)

    def compute(q):
        for b in range(2):
            queries_ = q2[b, :, lanes(q * LANES, LANES)]
            wide = queries_.astype(F32)
            masked = jnp.concatenate(
                [jnp.where(first, wide, 0.0), jnp.where(first, 0.0, wide)], axis=0
            ).astype(BF16)
            logits = dot_nt(masked, kbuf[q, b])
            weights = (logits + logits * jnp.tanh(logits)).astype(BF16)
            outs = dot(weights, vbuf[q, b])
            count = YS * zs * SLOTS
            out = jnp.where(first, outs[:count], outs[count:])
            pf[:, :, b * SLOTS:(b + 1) * SLOTS, :] = out.reshape(YS, zs, SLOTS, LANES)
        psend[q] = pf[...].astype(BF16)
        pown[q] = pf[y]
        for d in range(1, YS):
            py_copy(q, d).start()

    def reduce_y(q):
        settle(yrecv.at[q], py_recv.at[q])
        total_ = pown[q]
        for d in range(1, YS):
            total_ = total_ + yrecv[q, d - 1].astype(F32)
        pown[q] = total_
        zsend[q] = total_.astype(BF16)
        zown[q] = pown[q, z]
        for d in range(1, zs):
            pz_copy(q, d).start()

    def step(q, carry):
        compute(q)
        return carry

    lax.fori_loop(0, CHUNKS, step, 0)

    x_copy.wait_send()
    m_copy.wait_send()

    @pl.when(holds)
    def _():
        for j in range(2):
            for high in range(2):
                wx_copy(j, high, 1).wait_send()
                wx_copy(j, high, XS - 1).wait_send()
                wf_copy(j, 1 - own_kv, high).wait_send()

    @pl.when(jnp.logical_not(holds))
    def _():
        for j in range(2):
            for high in range(2):
                wh_copy(j, 0, high).wait_send()
                for kv in range(2):
                    wf_copy(j, kv, high).wait_send()

    for d in range(1, zs):
        qz_copy(d).wait_send()
    settle(others, qy_send.at[0])
    settle(csy, cy_send.at[0])

    settle(csz, cz_recv.at[0])
    packed = cs[1]
    for d in range(1, zs):
        packed = packed + csz[d - 1]
    summed = jnp.concatenate(
        [packed[2 * i:2 * i + 2] for i in range(half // LANES)], axis=1
    )
    summed = jnp.concatenate([summed, jnp.zeros((6, half), F32)], axis=0)
    l_avg.wait()
    part1 = summed.astype(BF16)
    rest = summed - part1.astype(F32)
    part2 = rest.astype(BF16)
    part3 = (rest - part2.astype(F32)).astype(BF16)
    pool[0] = dot(part1, avg[...]) + dot(part2, avg[...]) + dot(part3, avg[...])
    cp_copy = remote(pool.at[0], pool.at[1], cp_sem.at[0], cp_sem.at[1], sibling)
    cp_copy.start()

    def after(q, carry):
        reduce_y(q)
        return carry

    lax.fori_loop(0, CHUNKS, after, 0)

    def drain(q, carry):
        settle(yrecv.at[q], py_send.at[q])
        return carry

    lax.fori_loop(0, CHUNKS, drain, 0)
    settle(csz, cz_send.at[0])

    def reduce_z(q, carry):
        total_ = zown[q]
        settle(zrecv.at[q], pz_recv.at[q])
        for d in range(1, zs):
            total_ = total_ + zrecv[q, d - 1].astype(F32)
        afull[c, q] = total_
        return carry

    lax.fori_loop(0, CHUNKS, reduce_z, 0)
    a_copy = remote(afull.at[c], afull.at[c], a_sem.at[0], a_sem.at[1], sibling)
    a_copy.start()

    def drain_z(q, carry):
        settle(zrecv.at[q], pz_send.at[q])
        return carry

    lax.fori_loop(0, CHUNKS, drain_z, 0)

    cp_copy.wait()
    pooled = pool[0] + pool[1]
    for b in range(2):
        scale = 1.0 / (
            jnp.sqrt(jnp.full((8, LANES), ext_ref[b], jnp.int32).astype(F32)) * math.sqrt(half)
        )
        scores = lax.dot_general(
            pooled, pre[b], (((1,), (1,)), ((), ())),
            precision=lax.Precision.HIGHEST, preferred_element_type=F32,
        )
        coarse_ref[b:b + 1, :] = (scores * scale)[b:b + 1, :]

    a_copy.wait_recv()
    attention = jnp.concatenate(
        [afull[core, q] for core in range(CORES) for q in range(CHUNKS)], axis=1
    )
    width = 2 * half
    mean = jnp.sum(attention, axis=-1, keepdims=True) * (1.0 / width)
    centred = attention - mean
    variance = jnp.sum(centred * centred, axis=-1, keepdims=True) * (1.0 / width)
    normed = centred / jnp.sqrt(variance + epsilon)
    chosen_rows = xrow[...].astype(F32) + xbuf[...].astype(F32)
    mixed_ref[...] = (normed * gates[...] + chosen_rows).astype(BF16)
    a_copy.wait_send()


def place_kernel(scores_ref, mixed_ref, selt_ref, coarse_ref, fine_ref):
    coarse_ref[...] = scores_ref[...]
    for b in range(fine_ref.shape[0]):
        fine_ref[b] = dot(selt_ref[b], mixed_ref[...]).astype(BF16)


def local(memory, contenders, wc, wm, wco, avg, idx, ext):
    users, hist, width = memory.shape
    entries = contenders.shape[1]
    half = width // 2
    zs = lax.axis_size("seq") // (CORES * YS)
    slots = YS * zs * SLOTS
    dma = pltpu.SemaphoreType.DMA
    vmem = pltpu.VMEM
    any_ = pl.BlockSpec(memory_space=pl.ANY)
    scratch = [
        vmem((users, entries, width), BF16),
        vmem((width, half), BF16),
        vmem((width, width), BF16),
        vmem((width, width), BF16),
        vmem((half, half), BF16),
        vmem((users, CORES, hist, width), BF16),
        vmem((CHUNKS, 2, width, LANES), BF16),
        vmem((2 * SLOTS, width), BF16),
        vmem((2 * SLOTS, width), BF16),
        vmem((2 * SLOTS, width), F32),
        vmem((users, 2 * SLOTS, entries), BF16),
        vmem((YS, zs, 2 * SLOTS, half), BF16),
        vmem((users, slots, half), BF16),
        vmem((CHUNKS, users, CORES * hist, LANES), BF16),
        vmem((CHUNKS, users, CORES * hist, LANES), BF16),
        vmem((YS, zs, 2 * SLOTS, LANES), F32),
        vmem((CHUNKS, YS, zs, 2 * SLOTS, LANES), BF16),
        vmem((CHUNKS, zs, 2 * SLOTS, LANES), F32),
        vmem((CHUNKS, YS - 1, zs, 2 * SLOTS, LANES), BF16),
        vmem((CHUNKS, 2 * SLOTS, LANES), F32),
        vmem((CHUNKS, zs, 2 * SLOTS, LANES), BF16),
        vmem((CHUNKS, zs - 1, 2 * SLOTS, LANES), BF16),
        vmem((CORES, CHUNKS, 2 * SLOTS, LANES), F32),
        vmem((users, entries, half), F32),
        vmem((2, 8, LANES), F32),
        vmem((YS - 1, 8, LANES), F32),
        vmem((zs - 1, 8, LANES), F32),
        vmem((2, 8, half), F32),
        dma((6,)),
        dma((CHUNKS,)),
        dma((2,)),
        dma((2,)),
        dma((2, 2, 2)),
        dma((2, 2, 2)),
        dma((2, 2)),
        dma((2, 2)),
        dma((2, 2, 2)),
        dma((2, 2, 2)),
        dma((zs - 1,)),
        dma((zs - 1,)),
        dma((1,)),
        dma((1,)),
        dma((1,)),
        dma((1,)),
        dma((1,)),
        dma((1,)),
        dma((2,)),
        dma((CHUNKS,)),
        dma((CHUNKS,)),
        dma((CHUNKS,)),
        dma((CHUNKS,)),
        dma((2,)),
        pltpu.SemaphoreType.REGULAR((zs // 2, 2)),
    ]
    vm = pl.BlockSpec(memory_space=pltpu.VMEM)
    scores, mixed, selt = pl.pallas_call(
        functools.partial(kernel, zs),
        out_shape=(
            jax.ShapeDtypeStruct((users, entries), F32),
            jax.ShapeDtypeStruct((2 * SLOTS, width), BF16),
            jax.ShapeDtypeStruct((users, entries, 2 * SLOTS), BF16),
        ),
        in_specs=[any_] * 6
        + [pl.BlockSpec(memory_space=pltpu.VMEM), pl.BlockSpec(memory_space=pltpu.SMEM)],
        out_specs=(vm, vm, vm),
        scratch_shapes=scratch,
        compiler_params=pltpu.CompilerParams(
            collective_id=0, has_side_effects=True, vmem_limit_bytes=56 * 1024 * 1024
        ),
        cost_estimate=pl.CostEstimate(
            flops=6_500_000_000, bytes_accessed=12_000_000, transcendentals=7_000_000
        ),
    )(memory, contenders, wc, wm, wco, avg, idx, ext)
    return pl.pallas_call(
        place_kernel,
        out_shape=(
            jax.ShapeDtypeStruct((users, entries), F32),
            jax.ShapeDtypeStruct((users, entries, width), BF16),
        ),
        in_specs=[vm, vm, vm],
        out_specs=(vm, vm),
    )(scores, mixed, selt)


def solution(mesh):
    placed = (
        P("user", "seq", None),
        P("user", "seq", None),
        P(),
        P(None, "user"),
        P(),
        P(),
        P("user", None),
        P("user"),
    )
    return jax.shard_map(
        local,
        mesh=mesh,
        in_specs=placed,
        out_specs=(P("user", "seq"), P("user", "seq", None)),
        check_vma=False,
    )
```

```python
import functools
import math

import jax
import jax.numpy as jnp
from jax import lax
from jax.experimental import pallas as pl
from jax.experimental.pallas import tpu as pltpu
from jax.sharding import PartitionSpec as P

HEADS = 16
CORES = 2
YS = 4
XS = 4
CHUNKS = 4
LANES = 128
SLOTS = 8
epsilon = 1e-05

F32 = jnp.float32
BF16 = jnp.bfloat16
MESH = pl.DeviceIdType.MESH


def dot(a, b):
    return jnp.dot(a, b, preferred_element_type=F32)


def dot_nt(a, b):
    return lax.dot_general(a, b, (((1,), (1,)), ((), ())), preferred_element_type=F32)


def silu(x):
    h = x * 0.5
    return h + h * jnp.tanh(h)


def kernel(
    zs,
    m_hbm, cand_hbm, wc_hbm, wm_hbm, wco_hbm, avg_hbm, idx_ref, ext_ref,
    coarse_ref, mixed_ref, selt,
    cand, wq, wg, wco, avg, mall, wbuf,
    xbuf, xrow, gates, sel,
    qbuf, q2, kbuf, vbuf, pf, psend, pown, yrecv, zown, zsend, zrecv, afull,
    pre, cs, csy, csz, pool,
    local_sem, wl_sem, m_sem, x_sem, wx_send, wx_recv, wh_send, wh_recv, wf_send, wf_recv,
    qz_send, qz_recv, qy_send, qy_recv,
    cy_send, cy_recv, cz_send, cz_recv, cp_sem,
    py_send, py_recv, pz_send, pz_recv, a_sem, far_sem,
):
    u = lax.axis_index("user")
    s = lax.axis_index("seq")
    c = s % CORES
    y = (s // CORES) % YS
    z = s // (CORES * YS)
    chip = s // CORES
    hist = m_hbm.shape[1]
    half = wq.shape[1]
    colour = (y + z) % 2

    def at(x_, z_, y_, c_):
        return (x_, (z_ * YS + y_) * CORES + c_)

    sibling = at(u, z, y, 1 - c)

    def xpeer(d):
        return at((u + d) % XS, z, y, c)

    def ypeer(d):
        return at(u, z, (y + d) % YS, c)

    def zpeer(d):
        return at(u, (z + d) % zs, y, c)

    def lanes(start, size):
        return pl.ds(pl.multiple_of(start, LANES), size)

    def remote(src, dst, send, recv, device):
        return pltpu.make_async_remote_copy(
            src_ref=src, dst_ref=dst, send_sem=send, recv_sem=recv,
            device_id=device, device_id_type=MESH,
        )

    def settle(ref, sem):
        pltpu.make_async_copy(ref, ref, sem).wait()

    l_cand = pltpu.make_async_copy(cand_hbm, cand, local_sem.at[0])
    l_wq = pltpu.make_async_copy(
        wc_hbm.at[:, lanes(2 * half + c * half, half)], wq, local_sem.at[1]
    )
    l_m = pltpu.make_async_copy(m_hbm, mall.at[:, c], local_sem.at[2])
    l_wg = pltpu.make_async_copy(wc_hbm.at[:, pl.ds(0, 2 * half)], wg, local_sem.at[3])
    l_wco = pltpu.make_async_copy(wco_hbm, wco, local_sem.at[4])
    l_avg = pltpu.make_async_copy(
        avg_hbm.at[pl.ds(pl.multiple_of(c * half, half), half), :], avg, local_sem.at[5]
    )
    l_cand.start()
    l_wq.start()

    own_kv = u // 2
    holds = (u % 2) == c

    def wl_copy(q):
        return pltpu.make_async_copy(
            wm_hbm.at[:, lanes(q * LANES, LANES)], wbuf.at[q, own_kv], wl_sem.at[q]
        )

    @pl.when(holds)
    def _():
        for i in range(CHUNKS):
            wl_copy((2 * colour + i) % CHUNKS).start()

    barrier = pltpu.get_barrier_semaphore()

    def greet(device):
        pl.semaphore_signal(barrier, inc=1, device_id=device, device_id_type=MESH)

    greet(sibling)
    for peer, size in ((xpeer, XS), (ypeer, YS), (zpeer, zs)):
        greet(peer(1))
        greet(peer(size - 1))

    l_m.start()
    l_wg.start()
    l_wco.start()
    l_avg.start()

    rows16 = 2 * SLOTS
    ones = jnp.ones((rows16, idx_ref.shape[1]), BF16)
    pair = 2 * cand_hbm.shape[1]
    mine = cand_hbm.shape[1]
    upper = jnp.where(
        lax.broadcasted_iota(jnp.int32, (pair, pair), 0)
        < lax.broadcasted_iota(jnp.int32, (pair, pair), 1),
        1.0, 0.0,
    ).astype(BF16)
    eye = jnp.where(
        lax.broadcasted_iota(jnp.int32, (mine, mine), 0)
        == lax.broadcasted_iota(jnp.int32, (mine, mine), 1),
        1.0, 0.0,
    ).astype(BF16)
    row = lax.broadcasted_iota(jnp.int32, (rows16, pair), 0)
    for b in range(2):
        near = idx_ref[b:b + 1, :] - chip * pair
        matches = jnp.where(
            lax.broadcasted_iota(jnp.int32, (pair, idx_ref.shape[1]), 0) == near, 1.0, 0.0
        ).astype(BF16)
        flagged = dot_nt(ones, matches)
        placing = dot(flagged.astype(BF16), upper)
        target = (row - b * SLOTS).astype(F32)
        chosen = jnp.where((flagged > 0.5) & (jnp.abs(placing - target) < 0.5), 1.0, 0.0)
        chosen = jnp.where((row // SLOTS) == b, chosen, 0.0)
        own = jnp.where(c == 0, chosen[:, :mine], chosen[:, mine:]).astype(BF16)
        sel[b] = own
        selt[b] = dot_nt(eye, own).astype(BF16)

    l_cand.wait()
    found = dot(sel[0], cand[0]) + dot(sel[1], cand[1])
    xrow[...] = found.astype(BF16)

    pl.semaphore_wait(barrier, 7)

    def tell(r, peer, size):
        for side, d in ((0, 1), (1, size - 1)):
            pl.semaphore_signal(
                far_sem.at[r, side], inc=1, device_id=peer(d), device_id_type=MESH
            )

    def hear(r):
        for side in range(2):
            pl.semaphore_wait(far_sem.at[r, side], 1)

    rounds = zs // 2 - 1
    tell(0, zpeer, zs)
    tell(rounds, ypeer, YS)

    x_copy = remote(xrow, xbuf, x_sem.at[0], x_sem.at[1], sibling)
    x_copy.start()

    m_copy = remote(m_hbm, mall.at[:, c], m_sem.at[0], m_sem.at[1], sibling)
    m_copy.start()

    depth = wbuf.shape[2] // 2

    def part(q, kv, high):
        return wbuf.at[q, kv, pl.ds(pl.multiple_of(high * depth, depth), depth)]

    def wx_copy(j, high, d):
        half_ = part(2 * colour + j, own_kv, high)
        return remote(
            half_, half_, wx_send.at[j, high, d // 2], wx_recv.at[j, high, own_kv], xpeer(d)
        )

    @pl.when(holds)
    def _():
        for i in range(2):
            for j in range(2):
                if i == 0:
                    wl_copy(2 * colour + j).wait()
                wx_copy(j, i, 1).start()
                wx_copy(j, 1 - i, XS - 1).start()

    def wh_copy(j, kv, high):
        half_ = part(2 * colour + j, kv, high)
        return remote(
            half_, half_, wh_send.at[j, high], wh_recv.at[j, high],
            xpeer(1 + high * (XS - 2)),
        )

    def wf_copy(j, kv, high):
        half_ = part(2 * colour + j, kv, high)
        on_y = (kv == 0) if j == 0 else False
        y_peer = ypeer(1 + high * (YS - 2))
        z_peer = zpeer(1 + high * (zs - 2))
        device = (u, jnp.where(on_y, y_peer[1], z_peer[1]))
        return remote(
            half_, half_, wf_send.at[j, kv, high], wf_recv.at[j, kv, high], device
        )

    def near_relay(i, j):
        @pl.when(jnp.logical_not(holds))
        def _():
            for kv in range(2):
                behind = (c + 2 * kv + 1) % XS == u
                high = jnp.where(behind, i, 1 - i)
                half_ = part(2 * colour + j, kv, high)
                remote(
                    half_, half_, wx_send.at[j, high, 0], wx_recv.at[j, high, kv], xpeer(1)
                ).wait_recv()
                if i == 0:
                    wh_copy(j, kv, high).start()
                wf_copy(j, kv, high).start()

    def far_relay(j):
        @pl.when(holds)
        def _():
            for high in range(2):
                half_ = part(2 * colour + j, 1 - own_kv, high)
                remote(
                    half_, half_, wh_send.at[j, high], wh_recv.at[j, high], xpeer(1)
                ).wait_recv()
                wf_copy(j, 1 - own_kv, high).start()

    hear(0)
    tell(1, zpeer, zs)
    x_copy.wait_recv()
    for r in range(1, rounds - 1):
        hear(r)
        tell(r + 1, zpeer, zs)
    rows = xrow[...].astype(F32) + xbuf[...].astype(F32)
    xrow2 = rows.astype(BF16)
    l_wq.wait()
    queries = silu(dot(xrow2, wq[...])).astype(BF16)
    qbuf[y, z] = (queries.astype(F32) * (0.5 / math.sqrt(2 * half // HEADS))).astype(BF16)

    def qz_copy(d):
        return remote(qbuf.at[y, z], qbuf.at[y, z], qz_send.at[d - 1], qz_recv.at[d - 1], zpeer(d))

    def qy_copy(d, e):
        block = qbuf.at[y, (z - d + zs) % zs]
        return remote(block, block, qy_send.at[0], qy_recv.at[0], ypeer(e))

    def qy_relay(d):
        if d > 0:
            qz_copy(d).wait_recv()
        for e in range(1, YS):
            qy_copy(d, e).start()

    hear(rounds - 1)
    for d in sorted(range(1, zs), key=lambda d: -min(d, zs - d)):
        qz_copy(d).start()
    hear(rounds)
    qy_relay(0)
    near_relay(0, 0)
    near_relay(0, 1)
    qy_relay(1)
    qy_relay(zs - 1)
    near_relay(1, 0)
    near_relay(1, 1)
    far_relay(0)
    far_relay(1)
    qy_relay(2)
    qy_relay(zs - 2)
    for d in range(3, zs - 2):
        qy_relay(d)

    l_m.wait()
    m_copy.wait_recv()
    both = CORES * hist
    spot = chip * both + lax.broadcasted_iota(jnp.int32, (both, LANES), 0)

    def project(q):
        def block(b, carry):
            weights = jnp.concatenate([wbuf[q, 0], wbuf[q, 1]], axis=1)
            raw = dot(mall[b].reshape(both, 2 * half), weights)
            kbuf[q, b] = silu(raw[:, :LANES]).astype(BF16)
            vbuf[q, b] = jnp.where(spot < ext_ref[b], raw[:, LANES:], 0.0).astype(BF16)
            return carry

        lax.fori_loop(0, 2, block, 0)

    def own_chunk(j, carry):
        project(2 * colour + j)
        return carry

    lax.fori_loop(0, 2, own_chunk, 0)

    live_row = lax.broadcasted_iota(jnp.int32, (rows16, hist), 0)
    live_col = lax.broadcasted_iota(jnp.int32, (rows16, hist), 1)
    total = jnp.zeros((rows16, half), F32)
    for b in range(2):
        for core in range(CORES):
            place = (chip * CORES + core) * hist + live_col
            mask = jnp.where((live_row == b) & (place < ext_ref[b]), 1.0, 0.0).astype(BF16)
            total = total + dot(mask, mall[b, core, :, lanes(c * half, half)])
    cs[0] = jnp.concatenate(
        [total[:2, i * LANES:(i + 1) * LANES] for i in range(half // LANES)], axis=0
    )

    def cy_copy(d):
        return remote(cs.at[0], csy.at[d - 1], cy_send.at[0], cy_recv.at[0], ypeer(d))

    def cz_copy(d):
        return remote(cs.at[1], csz.at[d - 1], cz_send.at[0], cz_recv.at[0], zpeer(d))

    for d in range(1, YS):
        cy_copy(d).start()

    for j in range(2):
        other = 2 * (1 - colour) + j
        for kv in range(2):
            @pl.when(c + 2 * kv == u)
            def _():
                wl_copy(other).wait()

            @pl.when(c + 2 * kv != u)
            def _():
                for high in range(2):
                    half_ = part(other, kv, high)
                    remote(
                        half_, half_, wf_send.at[j, kv, high], wf_recv.at[j, kv, high], ypeer(1)
                    ).wait_recv()

        project(other)

    others = qbuf.at[pl.ds(0, YS - 1)]
    settle(others, qy_recv.at[0])
    for yy in range(YS):
        block = qbuf[yy].astype(F32)
        for b in range(2):
            own_rows = block[:, b * SLOTS:(b + 1) * SLOTS, :].reshape(zs * SLOTS, half)
            q2[b, yy * zs * SLOTS:(yy + 1) * zs * SLOTS, :] = own_rows.astype(BF16)

    settle(csy, cy_recv.at[0])
    cs[1] = cs[0] + (csy[0] + csy[1] + csy[2])
    for d in range(1, zs):
        cz_copy(d).start()

    def py_copy(q, d):
        return remote(
            psend.at[q, (y + d) % YS], yrecv.at[q, d - 1],
            py_send.at[q], py_recv.at[q], ypeer(d),
        )

    def pz_copy(q, d):
        return remote(
            zsend.at[q, (z + d) % zs], zrecv.at[q, d - 1],
            pz_send.at[q], pz_recv.at[q], zpeer(d),
        )

    lane = lax.broadcasted_iota(jnp.int32, (YS * zs * SLOTS, LANES), 1)
    first = lane < (LANES // 2)

    def compute(q):
        for b in range(2):
            queries_ = q2[b, :, lanes(q * LANES, LANES)]
            wide = queries_.astype(F32)
            masked = jnp.concatenate(
                [jnp.where(first, wide, 0.0), jnp.where(first, 0.0, wide)], axis=0
            ).astype(BF16)
            logits = dot_nt(masked, kbuf[q, b])
            weights = (logits + logits * jnp.tanh(logits)).astype(BF16)
            outs = dot(weights, vbuf[q, b])
            count = YS * zs * SLOTS
            out = jnp.where(first, outs[:count], outs[count:])
            pf[:, :, b * SLOTS:(b + 1) * SLOTS, :] = out.reshape(YS, zs, SLOTS, LANES)
        psend[q] = pf[...].astype(BF16)
        pown[q] = pf[y]
        for d in range(1, YS):
            py_copy(q, d).start()

    def reduce_y(q):
        settle(yrecv.at[q], py_recv.at[q])
        total_ = pown[q]
        for d in range(1, YS):
            total_ = total_ + yrecv[q, d - 1].astype(F32)
        pown[q] = total_
        zsend[q] = total_.astype(BF16)
        zown[q] = pown[q, z]
        for d in range(1, zs):
            pz_copy(q, d).start()

    def step(q, carry):
        compute(q)
        return carry

    lax.fori_loop(0, CHUNKS, step, 0)

    x_copy.wait_send()
    m_copy.wait_send()

    @pl.when(holds)
    def _():
        for j in range(2):
            for high in range(2):
                wx_copy(j, high, 1).wait_send()
                wx_copy(j, high, XS - 1).wait_send()
                wf_copy(j, 1 - own_kv, high).wait_send()

    @pl.when(jnp.logical_not(holds))
    def _():
        for j in range(2):
            for high in range(2):
                wh_copy(j, 0, high).wait_send()
                for kv in range(2):
                    wf_copy(j, kv, high).wait_send()

    for d in range(1, zs):
        qz_copy(d).wait_send()
    settle(others, qy_send.at[0])
    settle(csy, cy_send.at[0])

    l_wco.wait()
    for b in range(2):
        hidden = dot(cand[b], wco[...])
        pre[b] = silu(hidden[:, :half]) * hidden[:, half:]

    settle(csz, cz_recv.at[0])
    packed = cs[1]
    for d in range(1, zs):
        packed = packed + csz[d - 1]
    summed = jnp.concatenate(
        [packed[2 * i:2 * i + 2] for i in range(half // LANES)], axis=1
    )
    summed = jnp.concatenate([summed, jnp.zeros((6, half), F32)], axis=0)
    l_avg.wait()
    part1 = summed.astype(BF16)
    rest = summed - part1.astype(F32)
    part2 = rest.astype(BF16)
    part3 = (rest - part2.astype(F32)).astype(BF16)
    pool[0] = dot(part1, avg[...]) + dot(part2, avg[...]) + dot(part3, avg[...])
    cp_copy = remote(pool.at[0], pool.at[1], cp_sem.at[0], cp_sem.at[1], sibling)
    cp_copy.start()

    def after(q, carry):
        reduce_y(q)
        return carry

    lax.fori_loop(0, CHUNKS, after, 0)

    l_wg.wait()
    chosen_rows = xrow[...].astype(F32) + xbuf[...].astype(F32)
    gates[...] = silu(dot(chosen_rows.astype(BF16), wg[...]))

    def drain(q, carry):
        settle(yrecv.at[q], py_send.at[q])
        return carry

    lax.fori_loop(0, CHUNKS, drain, 0)
    settle(csz, cz_send.at[0])

    def reduce_z(q, carry):
        total_ = zown[q]
        settle(zrecv.at[q], pz_recv.at[q])
        for d in range(1, zs):
            total_ = total_ + zrecv[q, d - 1].astype(F32)
        afull[c, q] = total_
        return carry

    lax.fori_loop(0, CHUNKS, reduce_z, 0)
    a_copy = remote(afull.at[c], afull.at[c], a_sem.at[0], a_sem.at[1], sibling)
    a_copy.start()

    def drain_z(q, carry):
        settle(zrecv.at[q], pz_send.at[q])
        return carry

    lax.fori_loop(0, CHUNKS, drain_z, 0)

    cp_copy.wait()
    pooled = pool[0] + pool[1]
    for b in range(2):
        scale = 1.0 / (
            jnp.sqrt(jnp.full((8, LANES), ext_ref[b], jnp.int32).astype(F32)) * math.sqrt(half)
        )
        scores = lax.dot_general(
            pooled, pre[b], (((1,), (1,)), ((), ())),
            precision=lax.Precision.HIGHEST, preferred_element_type=F32,
        )
        coarse_ref[b:b + 1, :] = (scores * scale)[b:b + 1, :]

    a_copy.wait_recv()
    attention = jnp.concatenate(
        [afull[core, q] for core in range(CORES) for q in range(CHUNKS)], axis=1
    )
    width = 2 * half
    mean = jnp.sum(attention, axis=-1, keepdims=True) * (1.0 / width)
    centred = attention - mean
    variance = jnp.sum(centred * centred, axis=-1, keepdims=True) * (1.0 / width)
    normed = centred / jnp.sqrt(variance + epsilon)
    chosen_rows = xrow[...].astype(F32) + xbuf[...].astype(F32)
    mixed_ref[...] = (normed * gates[...] + chosen_rows).astype(BF16)
    a_copy.wait_send()


def place_kernel(scores_ref, mixed_ref, selt_ref, coarse_ref, fine_ref):
    coarse_ref[...] = scores_ref[...]
    for b in range(fine_ref.shape[0]):
        fine_ref[b] = dot(selt_ref[b], mixed_ref[...]).astype(BF16)


def local(memory, contenders, wc, wm, wco, avg, idx, ext):
    users, hist, width = memory.shape
    entries = contenders.shape[1]
    half = width // 2
    zs = lax.axis_size("seq") // (CORES * YS)
    slots = YS * zs * SLOTS
    dma = pltpu.SemaphoreType.DMA
    vmem = pltpu.VMEM
    any_ = pl.BlockSpec(memory_space=pl.ANY)
    scratch = [
        vmem((users, entries, width), BF16),
        vmem((width, half), BF16),
        vmem((width, width), BF16),
        vmem((width, width), BF16),
        vmem((half, half), BF16),
        vmem((users, CORES, hist, width), BF16),
        vmem((CHUNKS, 2, width, LANES), BF16),
        vmem((2 * SLOTS, width), BF16),
        vmem((2 * SLOTS, width), BF16),
        vmem((2 * SLOTS, width), F32),
        vmem((users, 2 * SLOTS, entries), BF16),
        vmem((YS, zs, 2 * SLOTS, half), BF16),
        vmem((users, slots, half), BF16),
        vmem((CHUNKS, users, CORES * hist, LANES), BF16),
        vmem((CHUNKS, users, CORES * hist, LANES), BF16),
        vmem((YS, zs, 2 * SLOTS, LANES), F32),
        vmem((CHUNKS, YS, zs, 2 * SLOTS, LANES), BF16),
        vmem((CHUNKS, zs, 2 * SLOTS, LANES), F32),
        vmem((CHUNKS, YS - 1, zs, 2 * SLOTS, LANES), BF16),
        vmem((CHUNKS, 2 * SLOTS, LANES), F32),
        vmem((CHUNKS, zs, 2 * SLOTS, LANES), BF16),
        vmem((CHUNKS, zs - 1, 2 * SLOTS, LANES), BF16),
        vmem((CORES, CHUNKS, 2 * SLOTS, LANES), F32),
        vmem((users, entries, half), F32),
        vmem((2, 8, LANES), F32),
        vmem((YS - 1, 8, LANES), F32),
        vmem((zs - 1, 8, LANES), F32),
        vmem((2, 8, half), F32),
        dma((6,)),
        dma((CHUNKS,)),
        dma((2,)),
        dma((2,)),
        dma((2, 2, 2)),
        dma((2, 2, 2)),
        dma((2, 2)),
        dma((2, 2)),
        dma((2, 2, 2)),
        dma((2, 2, 2)),
        dma((zs - 1,)),
        dma((zs - 1,)),
        dma((1,)),
        dma((1,)),
        dma((1,)),
        dma((1,)),
        dma((1,)),
        dma((1,)),
        dma((2,)),
        dma((CHUNKS,)),
        dma((CHUNKS,)),
        dma((CHUNKS,)),
        dma((CHUNKS,)),
        dma((2,)),
        pltpu.SemaphoreType.REGULAR((zs // 2, 2)),
    ]
    vm = pl.BlockSpec(memory_space=pltpu.VMEM)
    scores, mixed, selt = pl.pallas_call(
        functools.partial(kernel, zs),
        out_shape=(
            jax.ShapeDtypeStruct((users, entries), F32),
            jax.ShapeDtypeStruct((2 * SLOTS, width), BF16),
            jax.ShapeDtypeStruct((users, entries, 2 * SLOTS), BF16),
        ),
        in_specs=[any_] * 6
        + [pl.BlockSpec(memory_space=pltpu.VMEM), pl.BlockSpec(memory_space=pltpu.SMEM)],
        out_specs=(vm, vm, vm),
        scratch_shapes=scratch,
        compiler_params=pltpu.CompilerParams(
            collective_id=0, has_side_effects=True, vmem_limit_bytes=56 * 1024 * 1024
        ),
        cost_estimate=pl.CostEstimate(
            flops=6_500_000_000, bytes_accessed=12_000_000, transcendentals=7_000_000
        ),
    )(memory, contenders, wc, wm, wco, avg, idx, ext)
    return pl.pallas_call(
        place_kernel,
        out_shape=(
            jax.ShapeDtypeStruct((users, entries), F32),
            jax.ShapeDtypeStruct((users, entries, width), BF16),
        ),
        in_specs=[vm, vm, vm],
        out_specs=(vm, vm),
    )(scores, mixed, selt)


def solution(mesh):
    placed = (
        P("user", "seq", None),
        P("user", "seq", None),
        P(),
        P(None, "user"),
        P(),
        P(),
        P("user", None),
        P("user"),
    )
    return jax.shard_map(
        local,
        mesh=mesh,
        in_specs=placed,
        out_specs=(P("user", "seq"), P("user", "seq", None)),
        check_vma=False,
    )
```

```python
import functools
import math

import jax
import jax.numpy as jnp
from jax import lax
from jax.experimental import pallas as pl
from jax.experimental.pallas import tpu as pltpu
from jax.sharding import PartitionSpec as P

HEADS = 16
CORES = 2
YS = 4
XS = 4
CHUNKS = 4
LANES = 128
SLOTS = 8
epsilon = 1e-05

F32 = jnp.float32
BF16 = jnp.bfloat16
MESH = pl.DeviceIdType.MESH


def dot(a, b):
    return jnp.dot(a, b, preferred_element_type=F32)


def dot_nt(a, b):
    return lax.dot_general(a, b, (((1,), (1,)), ((), ())), preferred_element_type=F32)


def silu(x):
    h = x * 0.5
    return h + h * jnp.tanh(h)


def kernel(
    zs,
    m_hbm, cand_hbm, wc_hbm, wm_hbm, wco_hbm, avg_hbm, idx_ref, ext_ref,
    coarse_ref, mixed_ref, selt,
    cand, wq, wg, wco, avg, mall, wbuf,
    xbuf, xrow, gates, sel,
    qbuf, q2, kbuf, vbuf, pf, psend, pown, yrecv, zown, zsend, zrecv, afull,
    pre, cs, csy, csz, pool,
    local_sem, wl_sem, m_sem, x_sem, wx_send, wx_recv, wh_send, wh_recv, wf_send, wf_recv,
    qz_send, qz_recv, qy_send, qy_recv,
    cy_send, cy_recv, cz_send, cz_recv, cp_sem,
    py_send, py_recv, pz_send, pz_recv, a_sem, far_sem,
):
    u = lax.axis_index("user")
    s = lax.axis_index("seq")
    c = s % CORES
    y = (s // CORES) % YS
    z = s // (CORES * YS)
    chip = s // CORES
    hist = m_hbm.shape[1]
    half = wq.shape[1]
    colour = (y + z) % 2

    def at(x_, z_, y_, c_):
        return (x_, (z_ * YS + y_) * CORES + c_)

    sibling = at(u, z, y, 1 - c)

    def xpeer(d):
        return at((u + d) % XS, z, y, c)

    def ypeer(d):
        return at(u, z, (y + d) % YS, c)

    def zpeer(d):
        return at(u, (z + d) % zs, y, c)

    def lanes(start, size):
        return pl.ds(pl.multiple_of(start, LANES), size)

    def remote(src, dst, send, recv, device):
        return pltpu.make_async_remote_copy(
            src_ref=src, dst_ref=dst, send_sem=send, recv_sem=recv,
            device_id=device, device_id_type=MESH,
        )

    far_first = sorted(range(1, zs), key=lambda d: -min(d, zs - d))

    def settle(ref, sem):
        pltpu.make_async_copy(ref, ref, sem).wait()

    l_cand = pltpu.make_async_copy(cand_hbm, cand, local_sem.at[0])
    l_wq = pltpu.make_async_copy(
        wc_hbm.at[:, lanes(2 * half + c * half, half)], wq, local_sem.at[1]
    )
    l_m = pltpu.make_async_copy(m_hbm, mall.at[:, c], local_sem.at[2])
    l_wg = pltpu.make_async_copy(wc_hbm.at[:, pl.ds(0, 2 * half)], wg, local_sem.at[3])
    l_wco = pltpu.make_async_copy(wco_hbm, wco, local_sem.at[4])
    l_avg = pltpu.make_async_copy(
        avg_hbm.at[pl.ds(pl.multiple_of(c * half, half), half), :], avg, local_sem.at[5]
    )
    l_cand.start()
    l_wq.start()

    own_kv = u // 2
    holds = (u % 2) == c

    def wl_copy(q):
        return pltpu.make_async_copy(
            wm_hbm.at[:, lanes(q * LANES, LANES)], wbuf.at[q, own_kv], wl_sem.at[q]
        )

    @pl.when(holds)
    def _():
        for i in range(CHUNKS):
            wl_copy((2 * colour + i) % CHUNKS).start()

    barrier = pltpu.get_barrier_semaphore()

    def greet(device):
        pl.semaphore_signal(barrier, inc=1, device_id=device, device_id_type=MESH)

    greet(sibling)
    for peer, size in ((xpeer, XS), (ypeer, YS), (zpeer, zs)):
        greet(peer(1))
        greet(peer(size - 1))

    l_m.start()
    l_wg.start()
    l_wco.start()
    l_avg.start()

    pl.semaphore_wait(barrier, 7)

    def tell(r, peer, size):
        for side, d in ((0, 1), (1, size - 1)):
            pl.semaphore_signal(
                far_sem.at[r, side], inc=1, device_id=peer(d), device_id_type=MESH
            )

    def hear(r):
        for side in range(2):
            pl.semaphore_wait(far_sem.at[r, side], 1)

    rounds = zs // 2 - 1
    tell(0, zpeer, zs)
    tell(rounds, ypeer, YS)

    depth = wbuf.shape[2] // 2

    def part(q, kv, high):
        return wbuf.at[q, kv, pl.ds(pl.multiple_of(high * depth, depth), depth)]

    def wx_copy(j, high, d):
        half_ = part(2 * colour + j, own_kv, high)
        return remote(
            half_, half_, wx_send.at[j, high, d // 2], wx_recv.at[j, high, own_kv], xpeer(d)
        )

    @pl.when(holds)
    def _():
        for i in range(2):
            for j in range(2):
                if i == 0:
                    wl_copy(2 * colour + j).wait()
                wx_copy(j, i, 1).start()
                wx_copy(j, 1 - i, XS - 1).start()

    rows16 = 2 * SLOTS
    ones = jnp.ones((rows16, idx_ref.shape[1]), BF16)
    pair = 2 * cand_hbm.shape[1]
    mine = cand_hbm.shape[1]
    upper = jnp.where(
        lax.broadcasted_iota(jnp.int32, (pair, pair), 0)
        < lax.broadcasted_iota(jnp.int32, (pair, pair), 1),
        1.0, 0.0,
    ).astype(BF16)
    eye = jnp.where(
        lax.broadcasted_iota(jnp.int32, (mine, mine), 0)
        == lax.broadcasted_iota(jnp.int32, (mine, mine), 1),
        1.0, 0.0,
    ).astype(BF16)
    row = lax.broadcasted_iota(jnp.int32, (rows16, pair), 0)
    for b in range(2):
        near = idx_ref[b:b + 1, :] - chip * pair
        matches = jnp.where(
            lax.broadcasted_iota(jnp.int32, (pair, idx_ref.shape[1]), 0) == near, 1.0, 0.0
        ).astype(BF16)
        flagged = dot_nt(ones, matches)
        placing = dot(flagged.astype(BF16), upper)
        target = (row - b * SLOTS).astype(F32)
        chosen = jnp.where((flagged > 0.5) & (jnp.abs(placing - target) < 0.5), 1.0, 0.0)
        chosen = jnp.where((row // SLOTS) == b, chosen, 0.0)
        own = jnp.where(c == 0, chosen[:, :mine], chosen[:, mine:]).astype(BF16)
        sel[b] = own
        selt[b] = dot_nt(eye, own).astype(BF16)

    l_cand.wait()
    found = dot(sel[0], cand[0]) + dot(sel[1], cand[1])
    xrow[...] = found.astype(BF16)

    x_copy = remote(xrow, xbuf, x_sem.at[0], x_sem.at[1], sibling)
    x_copy.start()

    m_copy = remote(m_hbm, mall.at[:, c], m_sem.at[0], m_sem.at[1], sibling)
    m_copy.start()

    def wh_copy(j, kv, high):
        half_ = part(2 * colour + j, kv, high)
        return remote(
            half_, half_, wh_send.at[j, high], wh_recv.at[j, high],
            xpeer(1 + high * (XS - 2)),
        )

    def wf_copy(j, kv, high):
        half_ = part(2 * colour + j, kv, high)
        on_y = (kv == 0) if j == 0 else False
        y_peer = ypeer(1 + high * (YS - 2))
        z_peer = zpeer(1 + high * (zs - 2))
        device = (u, jnp.where(on_y, y_peer[1], z_peer[1]))
        return remote(
            half_, half_, wf_send.at[j, kv, high], wf_recv.at[j, kv, high], device
        )

    def near_relay(i, j):
        @pl.when(jnp.logical_not(holds))
        def _():
            for kv in range(2):
                behind = (c + 2 * kv + 1) % XS == u
                high = jnp.where(behind, i, 1 - i)
                half_ = part(2 * colour + j, kv, high)
                remote(
                    half_, half_, wx_send.at[j, high, 0], wx_recv.at[j, high, kv], xpeer(1)
                ).wait_recv()
                if i == 0:
                    wh_copy(j, kv, high).start()
                wf_copy(j, kv, high).start()

    def far_relay(j):
        @pl.when(holds)
        def _():
            for high in range(2):
                half_ = part(2 * colour + j, 1 - own_kv, high)
                remote(
                    half_, half_, wh_send.at[j, high], wh_recv.at[j, high], xpeer(1)
                ).wait_recv()
                wf_copy(j, 1 - own_kv, high).start()

    hear(0)
    tell(1, zpeer, zs)
    x_copy.wait_recv()
    for r in range(1, rounds - 1):
        hear(r)
        tell(r + 1, zpeer, zs)
    rows = xrow[...].astype(F32) + xbuf[...].astype(F32)
    xrow2 = rows.astype(BF16)
    l_wq.wait()
    queries = silu(dot(xrow2, wq[...])).astype(BF16)
    qbuf[y, z] = (queries.astype(F32) * (0.5 / math.sqrt(2 * half // HEADS))).astype(BF16)

    def qz_copy(d):
        return remote(qbuf.at[y, z], qbuf.at[y, z], qz_send.at[d - 1], qz_recv.at[d - 1], zpeer(d))

    def qy_copy(d, e):
        block = qbuf.at[y, (z - d + zs) % zs]
        return remote(block, block, qy_send.at[0], qy_recv.at[0], ypeer(e))

    def qy_relay(d):
        if d > 0:
            qz_copy(d).wait_recv()
        for e in (2, 1, YS - 1):
            qy_copy(d, e).start()

    hear(rounds - 1)
    for d in far_first:
        qz_copy(d).start()
    hear(rounds)
    qy_relay(0)
    near_relay(0, 0)
    near_relay(0, 1)
    qy_relay(1)
    qy_relay(zs - 1)
    near_relay(1, 0)
    near_relay(1, 1)
    far_relay(0)
    far_relay(1)
    qy_relay(2)
    qy_relay(zs - 2)
    for d in range(3, zs - 2):
        qy_relay(d)

    l_m.wait()
    m_copy.wait_recv()
    both = CORES * hist
    spot = chip * both + lax.broadcasted_iota(jnp.int32, (both, LANES), 0)

    def project(q):
        def block(b, carry):
            weights = jnp.concatenate([wbuf[q, 0], wbuf[q, 1]], axis=1)
            raw = dot(mall[b].reshape(both, 2 * half), weights)
            kbuf[q, b] = silu(raw[:, :LANES]).astype(BF16)
            vbuf[q, b] = jnp.where(spot < ext_ref[b], raw[:, LANES:], 0.0).astype(BF16)
            return carry

        lax.fori_loop(0, 2, block, 0)

    def own_chunk(j, carry):
        project(2 * colour + j)
        return carry

    lax.fori_loop(0, 2, own_chunk, 0)

    live_row = lax.broadcasted_iota(jnp.int32, (rows16, hist), 0)
    live_col = lax.broadcasted_iota(jnp.int32, (rows16, hist), 1)
    total = jnp.zeros((rows16, half), F32)
    for b in range(2):
        for core in range(CORES):
            place = (chip * CORES + core) * hist + live_col
            mask = jnp.where((live_row == b) & (place < ext_ref[b]), 1.0, 0.0).astype(BF16)
            total = total + dot(mask, mall[b, core, :, lanes(c * half, half)])
    cs[0] = jnp.concatenate(
        [total[:2, i * LANES:(i + 1) * LANES] for i in range(half // LANES)], axis=0
    )

    def cy_copy(d):
        return remote(cs.at[0], csy.at[d - 1], cy_send.at[0], cy_recv.at[0], ypeer(d))

    def cz_copy(d):
        return remote(cs.at[1], csz.at[d - 1], cz_send.at[0], cz_recv.at[0], zpeer(d))

    for d in range(1, YS):
        cy_copy(d).start()

    for j in range(2):
        other = 2 * (1 - colour) + j
        for kv in range(2):
            @pl.when(c + 2 * kv == u)
            def _():
                wl_copy(other).wait()

            @pl.when(c + 2 * kv != u)
            def _():
                for high in range(2):
                    half_ = part(other, kv, high)
                    remote(
                        half_, half_, wf_send.at[j, kv, high], wf_recv.at[j, kv, high], ypeer(1)
                    ).wait_recv()

        project(other)

    others = qbuf.at[pl.ds(0, YS - 1)]
    settle(others, qy_recv.at[0])
    for yy in range(YS):
        block = qbuf[yy].astype(F32)
        for b in range(2):
            own_rows = block[:, b * SLOTS:(b + 1) * SLOTS, :].reshape(zs * SLOTS, half)
            q2[b, yy * zs * SLOTS:(yy + 1) * zs * SLOTS, :] = own_rows.astype(BF16)

    settle(csy, cy_recv.at[0])
    cs[1] = cs[0] + (csy[0] + csy[1] + csy[2])
    for d in range(1, zs):
        cz_copy(d).start()

    def py_copy(q, d):
        return remote(
            psend.at[q, (y + d) % YS], yrecv.at[q, d - 1],
            py_send.at[q], py_recv.at[q], ypeer(d),
        )

    def pz_copy(q, d):
        return remote(
            zsend.at[q, (z + d) % zs], zrecv.at[q, d - 1],
            pz_send.at[q], pz_recv.at[q], zpeer(d),
        )

    lane = lax.broadcasted_iota(jnp.int32, (YS * zs * SLOTS, LANES), 1)
    first = lane < (LANES // 2)

    def compute(q):
        for b in range(2):
            queries_ = q2[b, :, lanes(q * LANES, LANES)]
            wide = queries_.astype(F32)
            masked = jnp.concatenate(
                [jnp.where(first, wide, 0.0), jnp.where(first, 0.0, wide)], axis=0
            ).astype(BF16)
            logits = dot_nt(masked, kbuf[q, b])
            weights = (logits + logits * jnp.tanh(logits)).astype(BF16)
            outs = dot(weights, vbuf[q, b])
            count = YS * zs * SLOTS
            out = jnp.where(first, outs[:count], outs[count:])
            pf[:, :, b * SLOTS:(b + 1) * SLOTS, :] = out.reshape(YS, zs, SLOTS, LANES)
        psend[q] = pf[...].astype(BF16)
        pown[q] = pf[y]
        for d in (2, 1, YS - 1):
            py_copy(q, d).start()

    def reduce_y(q):
        settle(yrecv.at[q], py_recv.at[q])
        total_ = pown[q]
        for d in range(1, YS):
            total_ = total_ + yrecv[q, d - 1].astype(F32)
        pown[q] = total_
        zsend[q] = total_.astype(BF16)
        zown[q] = pown[q, z]
        for d in far_first:
            pz_copy(q, d).start()

    def step(q, carry):
        compute(q)
        return carry

    lax.fori_loop(0, CHUNKS, step, 0)

    x_copy.wait_send()
    m_copy.wait_send()

    @pl.when(holds)
    def _():
        for j in range(2):
            for high in range(2):
                wx_copy(j, high, 1).wait_send()
                wx_copy(j, high, XS - 1).wait_send()
                wf_copy(j, 1 - own_kv, high).wait_send()

    @pl.when(jnp.logical_not(holds))
    def _():
        for j in range(2):
            for high in range(2):
                wh_copy(j, 0, high).wait_send()
                for kv in range(2):
                    wf_copy(j, kv, high).wait_send()

    for d in range(1, zs):
        qz_copy(d).wait_send()
    settle(others, qy_send.at[0])
    settle(csy, cy_send.at[0])

    l_wco.wait()
    for b in range(2):
        hidden = dot(cand[b], wco[...])
        pre[b] = silu(hidden[:, :half]) * hidden[:, half:]

    settle(csz, cz_recv.at[0])
    packed = cs[1]
    for d in range(1, zs):
        packed = packed + csz[d - 1]
    summed = jnp.concatenate(
        [packed[2 * i:2 * i + 2] for i in range(half // LANES)], axis=1
    )
    summed = jnp.concatenate([summed, jnp.zeros((6, half), F32)], axis=0)
    l_avg.wait()
    part1 = summed.astype(BF16)
    rest = summed - part1.astype(F32)
    part2 = rest.astype(BF16)
    part3 = (rest - part2.astype(F32)).astype(BF16)
    pool[0] = dot(part1, avg[...]) + dot(part2, avg[...]) + dot(part3, avg[...])
    cp_copy = remote(pool.at[0], pool.at[1], cp_sem.at[0], cp_sem.at[1], sibling)
    cp_copy.start()

    def after(q, carry):
        reduce_y(q)
        return carry

    lax.fori_loop(0, CHUNKS, after, 0)

    l_wg.wait()
    chosen_rows = xrow[...].astype(F32) + xbuf[...].astype(F32)
    gates[...] = silu(dot(chosen_rows.astype(BF16), wg[...]))

    def drain(q, carry):
        settle(yrecv.at[q], py_send.at[q])
        return carry

    lax.fori_loop(0, CHUNKS, drain, 0)
    settle(csz, cz_send.at[0])

    def reduce_z(q, carry):
        total_ = zown[q]
        settle(zrecv.at[q], pz_recv.at[q])
        for d in range(1, zs):
            total_ = total_ + zrecv[q, d - 1].astype(F32)
        afull[c, q] = total_
        return carry

    lax.fori_loop(0, CHUNKS, reduce_z, 0)
    a_copy = remote(afull.at[c], afull.at[c], a_sem.at[0], a_sem.at[1], sibling)
    a_copy.start()

    def drain_z(q, carry):
        settle(zrecv.at[q], pz_send.at[q])
        return carry

    lax.fori_loop(0, CHUNKS, drain_z, 0)

    cp_copy.wait()
    pooled = pool[0] + pool[1]
    for b in range(2):
        scale = 1.0 / (
            jnp.sqrt(jnp.full((8, LANES), ext_ref[b], jnp.int32).astype(F32)) * math.sqrt(half)
        )
        scores = lax.dot_general(
            pooled, pre[b], (((1,), (1,)), ((), ())),
            precision=lax.Precision.HIGHEST, preferred_element_type=F32,
        )
        coarse_ref[b:b + 1, :] = (scores * scale)[b:b + 1, :]

    a_copy.wait_recv()
    attention = jnp.concatenate(
        [afull[core, q] for core in range(CORES) for q in range(CHUNKS)], axis=1
    )
    width = 2 * half
    mean = jnp.sum(attention, axis=-1, keepdims=True) * (1.0 / width)
    centred = attention - mean
    variance = jnp.sum(centred * centred, axis=-1, keepdims=True) * (1.0 / width)
    normed = centred / jnp.sqrt(variance + epsilon)
    chosen_rows = xrow[...].astype(F32) + xbuf[...].astype(F32)
    mixed_ref[...] = (normed * gates[...] + chosen_rows).astype(BF16)
    a_copy.wait_send()


def place_kernel(scores_ref, mixed_ref, selt_ref, coarse_ref, fine_ref):
    coarse_ref[...] = scores_ref[...]
    for b in range(fine_ref.shape[0]):
        fine_ref[b] = dot(selt_ref[b], mixed_ref[...]).astype(BF16)


def local(memory, contenders, wc, wm, wco, avg, idx, ext):
    users, hist, width = memory.shape
    entries = contenders.shape[1]
    half = width // 2
    zs = lax.axis_size("seq") // (CORES * YS)
    slots = YS * zs * SLOTS
    dma = pltpu.SemaphoreType.DMA
    vmem = pltpu.VMEM
    any_ = pl.BlockSpec(memory_space=pl.ANY)
    scratch = [
        vmem((users, entries, width), BF16),
        vmem((width, half), BF16),
        vmem((width, width), BF16),
        vmem((width, width), BF16),
        vmem((half, half), BF16),
        vmem((users, CORES, hist, width), BF16),
        vmem((CHUNKS, 2, width, LANES), BF16),
        vmem((2 * SLOTS, width), BF16),
        vmem((2 * SLOTS, width), BF16),
        vmem((2 * SLOTS, width), F32),
        vmem((users, 2 * SLOTS, entries), BF16),
        vmem((YS, zs, 2 * SLOTS, half), BF16),
        vmem((users, slots, half), BF16),
        vmem((CHUNKS, users, CORES * hist, LANES), BF16),
        vmem((CHUNKS, users, CORES * hist, LANES), BF16),
        vmem((YS, zs, 2 * SLOTS, LANES), F32),
        vmem((CHUNKS, YS, zs, 2 * SLOTS, LANES), BF16),
        vmem((CHUNKS, zs, 2 * SLOTS, LANES), F32),
        vmem((CHUNKS, YS - 1, zs, 2 * SLOTS, LANES), BF16),
        vmem((CHUNKS, 2 * SLOTS, LANES), F32),
        vmem((CHUNKS, zs, 2 * SLOTS, LANES), BF16),
        vmem((CHUNKS, zs - 1, 2 * SLOTS, LANES), BF16),
        vmem((CORES, CHUNKS, 2 * SLOTS, LANES), F32),
        vmem((users, entries, half), F32),
        vmem((2, 8, LANES), F32),
        vmem((YS - 1, 8, LANES), F32),
        vmem((zs - 1, 8, LANES), F32),
        vmem((2, 8, half), F32),
        dma((6,)),
        dma((CHUNKS,)),
        dma((2,)),
        dma((2,)),
        dma((2, 2, 2)),
        dma((2, 2, 2)),
        dma((2, 2)),
        dma((2, 2)),
        dma((2, 2, 2)),
        dma((2, 2, 2)),
        dma((zs - 1,)),
        dma((zs - 1,)),
        dma((1,)),
        dma((1,)),
        dma((1,)),
        dma((1,)),
        dma((1,)),
        dma((1,)),
        dma((2,)),
        dma((CHUNKS,)),
        dma((CHUNKS,)),
        dma((CHUNKS,)),
        dma((CHUNKS,)),
        dma((2,)),
        pltpu.SemaphoreType.REGULAR((zs // 2, 2)),
    ]
    vm = pl.BlockSpec(memory_space=pltpu.VMEM)
    scores, mixed, selt = pl.pallas_call(
        functools.partial(kernel, zs),
        out_shape=(
            jax.ShapeDtypeStruct((users, entries), F32),
            jax.ShapeDtypeStruct((2 * SLOTS, width), BF16),
            jax.ShapeDtypeStruct((users, entries, 2 * SLOTS), BF16),
        ),
        in_specs=[any_] * 6
        + [pl.BlockSpec(memory_space=pltpu.VMEM), pl.BlockSpec(memory_space=pltpu.SMEM)],
        out_specs=(vm, vm, vm),
        scratch_shapes=scratch,
        compiler_params=pltpu.CompilerParams(
            collective_id=0, has_side_effects=True, vmem_limit_bytes=56 * 1024 * 1024
        ),
        cost_estimate=pl.CostEstimate(
            flops=6_500_000_000, bytes_accessed=12_000_000, transcendentals=7_000_000
        ),
    )(memory, contenders, wc, wm, wco, avg, idx, ext)
    return pl.pallas_call(
        place_kernel,
        out_shape=(
            jax.ShapeDtypeStruct((users, entries), F32),
            jax.ShapeDtypeStruct((users, entries, width), BF16),
        ),
        in_specs=[vm, vm, vm],
        out_specs=(vm, vm),
    )(scores, mixed, selt)


def solution(mesh):
    placed = (
        P("user", "seq", None),
        P("user", "seq", None),
        P(),
        P(None, "user"),
        P(),
        P(),
        P("user", None),
        P("user"),
    )
    return jax.shard_map(
        local,
        mesh=mesh,
        in_specs=placed,
        out_specs=(P("user", "seq"), P("user", "seq", None)),
        check_vma=False,
    )
```

```python
import functools
import math

import jax
import jax.numpy as jnp
from jax import lax
from jax.experimental import pallas as pl
from jax.experimental.pallas import tpu as pltpu
from jax.sharding import PartitionSpec as P

HEADS = 16
CORES = 2
YS = 4
XS = 4
CHUNKS = 4
LANES = 128
SLOTS = 8
epsilon = 1e-05

F32 = jnp.float32
BF16 = jnp.bfloat16
MESH = pl.DeviceIdType.MESH


def dot(a, b):
    return jnp.dot(a, b, preferred_element_type=F32)


def dot_nt(a, b):
    return lax.dot_general(a, b, (((1,), (1,)), ((), ())), preferred_element_type=F32)


def silu(x):
    h = x * 0.5
    return h + h * jnp.tanh(h)


def kernel(
    zs,
    m_hbm, cand_hbm, wc_hbm, wm_hbm, wco_hbm, avg_hbm, idx_ref, ext_ref,
    coarse_ref, mixed_ref, selt,
    cand, wq, wg, wco, avg, mall, wbuf,
    xbuf, xrow, gates, sel,
    qbuf, q2, kbuf, vbuf, pf, psend, pown, yrecv, zown, zsend, zrecv, afull,
    pre, cs, csy, csz, pool,
    local_sem, wl_sem, m_sem, x_sem, wx_send, wx_recv, wh_send, wh_recv, wf_send, wf_recv,
    qz_send, qz_recv, qy_send, qy_recv,
    cy_send, cy_recv, cz_send, cz_recv, cp_sem,
    py_send, py_recv, pz_send, pz_recv, a_sem, far_sem,
):
    u = lax.axis_index("user")
    s = lax.axis_index("seq")
    c = s % CORES
    y = (s // CORES) % YS
    z = s // (CORES * YS)
    chip = s // CORES
    hist = m_hbm.shape[1]
    half = wq.shape[1]
    colour = (y + z) % 2

    def at(x_, z_, y_, c_):
        return (x_, (z_ * YS + y_) * CORES + c_)

    sibling = at(u, z, y, 1 - c)

    def xpeer(d):
        return at((u + d) % XS, z, y, c)

    def ypeer(d):
        return at(u, z, (y + d) % YS, c)

    def zpeer(d):
        return at(u, (z + d) % zs, y, c)

    def lanes(start, size):
        return pl.ds(pl.multiple_of(start, LANES), size)

    def remote(src, dst, send, recv, device):
        return pltpu.make_async_remote_copy(
            src_ref=src, dst_ref=dst, send_sem=send, recv_sem=recv,
            device_id=device, device_id_type=MESH,
        )

    far_first = sorted(range(1, zs), key=lambda d: -min(d, zs - d))

    def settle(ref, sem):
        pltpu.make_async_copy(ref, ref, sem).wait()

    l_cand = pltpu.make_async_copy(cand_hbm, cand, local_sem.at[0])
    l_wq = pltpu.make_async_copy(
        wc_hbm.at[:, lanes(2 * half + c * half, half)], wq, local_sem.at[1]
    )
    l_m = pltpu.make_async_copy(m_hbm, mall.at[:, c], local_sem.at[2])
    l_wg = pltpu.make_async_copy(wc_hbm.at[:, pl.ds(0, 2 * half)], wg, local_sem.at[3])
    l_wco = pltpu.make_async_copy(wco_hbm, wco, local_sem.at[4])
    l_avg = pltpu.make_async_copy(
        avg_hbm.at[pl.ds(pl.multiple_of(c * half, half), half), :], avg, local_sem.at[5]
    )
    l_cand.start()
    l_wq.start()

    own_kv = u // 2
    holds = (u % 2) == c

    def wl_copy(q):
        return pltpu.make_async_copy(
            wm_hbm.at[:, lanes(q * LANES, LANES)], wbuf.at[q, own_kv], wl_sem.at[q]
        )

    @pl.when(holds)
    def _():
        for i in range(CHUNKS):
            wl_copy((2 * colour + i) % CHUNKS).start()

    barrier = pltpu.get_barrier_semaphore()

    def greet(device):
        pl.semaphore_signal(barrier, inc=1, device_id=device, device_id_type=MESH)

    greet(sibling)
    for peer, size in ((xpeer, XS), (ypeer, YS), (zpeer, zs)):
        greet(peer(1))
        greet(peer(size - 1))

    l_m.start()
    l_wg.start()
    l_wco.start()
    l_avg.start()

    pl.semaphore_wait(barrier, 7)

    def tell(r, peer, size):
        for side, d in ((0, 1), (1, size - 1)):
            pl.semaphore_signal(
                far_sem.at[r, side], inc=1, device_id=peer(d), device_id_type=MESH
            )

    def hear(r):
        for side in range(2):
            pl.semaphore_wait(far_sem.at[r, side], 1)

    rounds = zs // 2 - 1
    tell(0, zpeer, zs)
    tell(rounds, ypeer, YS)

    depth = wbuf.shape[2] // 2

    def part(q, kv, high):
        return wbuf.at[q, kv, pl.ds(pl.multiple_of(high * depth, depth), depth)]

    def wx_copy(j, high, d):
        half_ = part(2 * colour + j, own_kv, high)
        return remote(
            half_, half_, wx_send.at[j, high, d // 2], wx_recv.at[j, high, own_kv], xpeer(d)
        )

    @pl.when(holds)
    def _():
        for i in range(2):
            for j in range(2):
                if i == 0:
                    wl_copy(2 * colour + j).wait()
                wx_copy(j, i, 1).start()
                wx_copy(j, 1 - i, XS - 1).start()

    rows16 = 2 * SLOTS
    ones = jnp.ones((rows16, idx_ref.shape[1]), BF16)
    pair = 2 * cand_hbm.shape[1]
    mine = cand_hbm.shape[1]
    upper = jnp.where(
        lax.broadcasted_iota(jnp.int32, (pair, pair), 0)
        < lax.broadcasted_iota(jnp.int32, (pair, pair), 1),
        1.0, 0.0,
    ).astype(BF16)
    eye = jnp.where(
        lax.broadcasted_iota(jnp.int32, (mine, mine), 0)
        == lax.broadcasted_iota(jnp.int32, (mine, mine), 1),
        1.0, 0.0,
    ).astype(BF16)
    row = lax.broadcasted_iota(jnp.int32, (rows16, pair), 0)
    for b in range(2):
        near = idx_ref[b:b + 1, :] - chip * pair
        matches = jnp.where(
            lax.broadcasted_iota(jnp.int32, (pair, idx_ref.shape[1]), 0) == near, 1.0, 0.0
        ).astype(BF16)
        flagged = dot_nt(ones, matches)
        placing = dot(flagged.astype(BF16), upper)
        target = (row - b * SLOTS).astype(F32)
        chosen = jnp.where((flagged > 0.5) & (jnp.abs(placing - target) < 0.5), 1.0, 0.0)
        chosen = jnp.where((row // SLOTS) == b, chosen, 0.0)
        own = jnp.where(c == 0, chosen[:, :mine], chosen[:, mine:]).astype(BF16)
        sel[b] = own
        selt[b] = dot_nt(eye, own).astype(BF16)

    l_cand.wait()
    found = dot(sel[0], cand[0]) + dot(sel[1], cand[1])
    xrow[...] = found.astype(BF16)

    x_copy = remote(xrow, xbuf, x_sem.at[0], x_sem.at[1], sibling)
    x_copy.start()

    m_copy = remote(m_hbm, mall.at[:, c], m_sem.at[0], m_sem.at[1], sibling)
    m_copy.start()

    def wh_copy(j, kv, high):
        half_ = part(2 * colour + j, kv, high)
        return remote(
            half_, half_, wh_send.at[j, high], wh_recv.at[j, high],
            xpeer(1 + high * (XS - 2)),
        )

    def wf_copy(j, kv, high):
        half_ = part(2 * colour + j, kv, high)
        on_y = (kv == 0) if j == 0 else False
        y_peer = ypeer(1 + high * (YS - 2))
        z_peer = zpeer(1 + high * (zs - 2))
        device = (u, jnp.where(on_y, y_peer[1], z_peer[1]))
        return remote(
            half_, half_, wf_send.at[j, kv, high], wf_recv.at[j, kv, high], device
        )

    def near_relay(i, j):
        @pl.when(jnp.logical_not(holds))
        def _():
            for kv in range(2):
                behind = (c + 2 * kv + 1) % XS == u
                high = jnp.where(behind, i, 1 - i)
                half_ = part(2 * colour + j, kv, high)
                remote(
                    half_, half_, wx_send.at[j, high, 0], wx_recv.at[j, high, kv], xpeer(1)
                ).wait_recv()
                if i == 0:
                    wh_copy(j, kv, high).start()
                wf_copy(j, kv, high).start()

    def far_relay(j):
        @pl.when(holds)
        def _():
            for high in range(2):
                half_ = part(2 * colour + j, 1 - own_kv, high)
                remote(
                    half_, half_, wh_send.at[j, high], wh_recv.at[j, high], xpeer(1)
                ).wait_recv()
                wf_copy(j, 1 - own_kv, high).start()

    hear(0)
    tell(1, zpeer, zs)
    x_copy.wait_recv()
    for r in range(1, rounds - 1):
        hear(r)
        tell(r + 1, zpeer, zs)
    rows = xrow[...].astype(F32) + xbuf[...].astype(F32)
    xrow2 = rows.astype(BF16)
    l_wq.wait()
    queries = silu(dot(xrow2, wq[...])).astype(BF16)
    qbuf[y, z] = (queries.astype(F32) * (0.5 / math.sqrt(2 * half // HEADS))).astype(BF16)

    def qz_copy(d):
        return remote(qbuf.at[y, z], qbuf.at[y, z], qz_send.at[d - 1], qz_recv.at[d - 1], zpeer(d))

    def qy_copy(d, e):
        block = qbuf.at[y, (z - d + zs) % zs]
        return remote(block, block, qy_send.at[0], qy_recv.at[0], ypeer(e))

    def qy_relay(d):
        if d > 0:
            qz_copy(d).wait_recv()
        for e in (2, 1, YS - 1):
            qy_copy(d, e).start()

    hear(rounds - 1)
    for d in far_first:
        qz_copy(d).start()
    hear(rounds)
    qy_relay(0)
    near_relay(0, 0)
    near_relay(0, 1)
    qy_relay(1)
    qy_relay(zs - 1)
    near_relay(1, 0)
    near_relay(1, 1)
    far_relay(0)
    far_relay(1)
    qy_relay(2)
    qy_relay(zs - 2)
    for d in range(3, zs - 2):
        qy_relay(d)

    l_m.wait()
    m_copy.wait_recv()
    both = CORES * hist
    spot = chip * both + lax.broadcasted_iota(jnp.int32, (both, LANES), 0)

    def project(q):
        def block(b, carry):
            weights = jnp.concatenate([wbuf[q, 0], wbuf[q, 1]], axis=1)
            raw = dot(mall[b].reshape(both, 2 * half), weights)
            kbuf[q, b] = silu(raw[:, :LANES]).astype(BF16)
            vbuf[q, b] = jnp.where(spot < ext_ref[b], raw[:, LANES:], 0.0).astype(BF16)
            return carry

        lax.fori_loop(0, 2, block, 0)

    def own_chunk(j, carry):
        project(2 * colour + j)
        return carry

    lax.fori_loop(0, 2, own_chunk, 0)

    live_row = lax.broadcasted_iota(jnp.int32, (rows16, hist), 0)
    live_col = lax.broadcasted_iota(jnp.int32, (rows16, hist), 1)
    total = jnp.zeros((rows16, half), F32)
    for b in range(2):
        for core in range(CORES):
            place = (chip * CORES + core) * hist + live_col
            mask = jnp.where((live_row == b) & (place < ext_ref[b]), 1.0, 0.0).astype(BF16)
            total = total + dot(mask, mall[b, core, :, lanes(c * half, half)])
    cs[0] = jnp.concatenate(
        [total[:2, i * LANES:(i + 1) * LANES] for i in range(half // LANES)], axis=0
    )

    def cy_copy(d):
        return remote(cs.at[0], csy.at[d - 1], cy_send.at[0], cy_recv.at[0], ypeer(d))

    def cz_copy(d):
        return remote(cs.at[1], csz.at[d - 1], cz_send.at[0], cz_recv.at[0], zpeer(d))

    for d in range(1, YS):
        cy_copy(d).start()

    for j in range(2):
        other = 2 * (1 - colour) + j
        for kv in range(2):
            @pl.when(c + 2 * kv == u)
            def _():
                wl_copy(other).wait()

            @pl.when(c + 2 * kv != u)
            def _():
                for high in range(2):
                    half_ = part(other, kv, high)
                    remote(
                        half_, half_, wf_send.at[j, kv, high], wf_recv.at[j, kv, high], ypeer(1)
                    ).wait_recv()

        project(other)

    others = qbuf.at[pl.ds(0, YS - 1)]
    settle(others, qy_recv.at[0])
    for yy in range(YS):
        block = qbuf[yy].astype(F32)
        for b in range(2):
            own_rows = block[:, b * SLOTS:(b + 1) * SLOTS, :].reshape(zs * SLOTS, half)
            q2[b, yy * zs * SLOTS:(yy + 1) * zs * SLOTS, :] = own_rows.astype(BF16)

    settle(csy, cy_recv.at[0])
    cs[1] = cs[0] + (csy[0] + csy[1] + csy[2])
    for d in range(1, zs):
        cz_copy(d).start()

    def py_copy(q, d):
        return remote(
            psend.at[q, (y + d) % YS], yrecv.at[q, d - 1],
            py_send.at[q], py_recv.at[q], ypeer(d),
        )

    def pz_copy(q, d):
        return remote(
            zsend.at[q, (z + d) % zs], zrecv.at[q, d - 1],
            pz_send.at[q], pz_recv.at[q], zpeer(d),
        )

    lane = lax.broadcasted_iota(jnp.int32, (YS * zs * SLOTS, LANES), 1)
    first = lane < (LANES // 2)

    def compute(q):
        for b in range(2):
            queries_ = q2[b, :, lanes(q * LANES, LANES)]
            wide = queries_.astype(F32)
            masked = jnp.concatenate(
                [jnp.where(first, wide, 0.0), jnp.where(first, 0.0, wide)], axis=0
            ).astype(BF16)
            logits = dot_nt(masked, kbuf[q, b])
            weights = (logits + logits * jnp.tanh(logits)).astype(BF16)
            outs = dot(weights, vbuf[q, b])
            count = YS * zs * SLOTS
            out = jnp.where(first, outs[:count], outs[count:])
            pf[:, :, b * SLOTS:(b + 1) * SLOTS, :] = out.reshape(YS, zs, SLOTS, LANES)
        psend[q] = pf[...].astype(BF16)
        pown[q] = pf[y]
        for d in (2, 1, YS - 1):
            py_copy(q, d).start()

    def reduce_y(q):
        settle(yrecv.at[q], py_recv.at[q])
        total_ = pown[q]
        for d in range(1, YS):
            total_ = total_ + yrecv[q, d - 1].astype(F32)
        pown[q] = total_
        zsend[q] = total_.astype(BF16)
        zown[q] = pown[q, z]
        for d in far_first:
            pz_copy(q, d).start()

    def step(q, carry):
        compute(q)
        return carry

    for q in range(CHUNKS):
        step(q, 0)

    x_copy.wait_send()
    m_copy.wait_send()

    @pl.when(holds)
    def _():
        for j in range(2):
            for high in range(2):
                wx_copy(j, high, 1).wait_send()
                wx_copy(j, high, XS - 1).wait_send()
                wf_copy(j, 1 - own_kv, high).wait_send()

    @pl.when(jnp.logical_not(holds))
    def _():
        for j in range(2):
            for high in range(2):
                wh_copy(j, 0, high).wait_send()
                for kv in range(2):
                    wf_copy(j, kv, high).wait_send()

    for d in range(1, zs):
        qz_copy(d).wait_send()
    settle(others, qy_send.at[0])
    settle(csy, cy_send.at[0])

    l_wco.wait()
    for b in range(2):
        hidden = dot(cand[b], wco[...])
        pre[b] = silu(hidden[:, :half]) * hidden[:, half:]

    settle(csz, cz_recv.at[0])
    packed = cs[1]
    for d in range(1, zs):
        packed = packed + csz[d - 1]
    summed = jnp.concatenate(
        [packed[2 * i:2 * i + 2] for i in range(half // LANES)], axis=1
    )
    summed = jnp.concatenate([summed, jnp.zeros((6, half), F32)], axis=0)
    l_avg.wait()
    part1 = summed.astype(BF16)
    rest = summed - part1.astype(F32)
    part2 = rest.astype(BF16)
    part3 = (rest - part2.astype(F32)).astype(BF16)
    pool[0] = dot(part1, avg[...]) + dot(part2, avg[...]) + dot(part3, avg[...])
    cp_copy = remote(pool.at[0], pool.at[1], cp_sem.at[0], cp_sem.at[1], sibling)
    cp_copy.start()

    def after(q, carry):
        reduce_y(q)
        return carry

    lax.fori_loop(0, CHUNKS, after, 0)

    l_wg.wait()
    chosen_rows = xrow[...].astype(F32) + xbuf[...].astype(F32)
    gates[...] = silu(dot(chosen_rows.astype(BF16), wg[...]))

    def drain(q, carry):
        settle(yrecv.at[q], py_send.at[q])
        return carry

    lax.fori_loop(0, CHUNKS, drain, 0)
    settle(csz, cz_send.at[0])

    def reduce_z(q, carry):
        total_ = zown[q]
        settle(zrecv.at[q], pz_recv.at[q])
        for d in range(1, zs):
            total_ = total_ + zrecv[q, d - 1].astype(F32)
        afull[c, q] = total_
        return carry

    lax.fori_loop(0, CHUNKS, reduce_z, 0)
    a_copy = remote(afull.at[c], afull.at[c], a_sem.at[0], a_sem.at[1], sibling)
    a_copy.start()

    def drain_z(q, carry):
        settle(zrecv.at[q], pz_send.at[q])
        return carry

    lax.fori_loop(0, CHUNKS, drain_z, 0)

    cp_copy.wait()
    pooled = pool[0] + pool[1]
    for b in range(2):
        scale = 1.0 / (
            jnp.sqrt(jnp.full((8, LANES), ext_ref[b], jnp.int32).astype(F32)) * math.sqrt(half)
        )
        scores = lax.dot_general(
            pooled, pre[b], (((1,), (1,)), ((), ())),
            precision=lax.Precision.HIGHEST, preferred_element_type=F32,
        )
        coarse_ref[b:b + 1, :] = (scores * scale)[b:b + 1, :]

    a_copy.wait_recv()
    attention = jnp.concatenate(
        [afull[core, q] for core in range(CORES) for q in range(CHUNKS)], axis=1
    )
    width = 2 * half
    mean = jnp.sum(attention, axis=-1, keepdims=True) * (1.0 / width)
    centred = attention - mean
    variance = jnp.sum(centred * centred, axis=-1, keepdims=True) * (1.0 / width)
    normed = centred / jnp.sqrt(variance + epsilon)
    chosen_rows = xrow[...].astype(F32) + xbuf[...].astype(F32)
    mixed_ref[...] = (normed * gates[...] + chosen_rows).astype(BF16)
    a_copy.wait_send()


def place_kernel(scores_ref, mixed_ref, selt_ref, coarse_ref, fine_ref):
    coarse_ref[...] = scores_ref[...]
    for b in range(fine_ref.shape[0]):
        fine_ref[b] = dot(selt_ref[b], mixed_ref[...]).astype(BF16)


def local(memory, contenders, wc, wm, wco, avg, idx, ext):
    users, hist, width = memory.shape
    entries = contenders.shape[1]
    half = width // 2
    zs = lax.axis_size("seq") // (CORES * YS)
    slots = YS * zs * SLOTS
    dma = pltpu.SemaphoreType.DMA
    vmem = pltpu.VMEM
    any_ = pl.BlockSpec(memory_space=pl.ANY)
    scratch = [
        vmem((users, entries, width), BF16),
        vmem((width, half), BF16),
        vmem((width, width), BF16),
        vmem((width, width), BF16),
        vmem((half, half), BF16),
        vmem((users, CORES, hist, width), BF16),
        vmem((CHUNKS, 2, width, LANES), BF16),
        vmem((2 * SLOTS, width), BF16),
        vmem((2 * SLOTS, width), BF16),
        vmem((2 * SLOTS, width), F32),
        vmem((users, 2 * SLOTS, entries), BF16),
        vmem((YS, zs, 2 * SLOTS, half), BF16),
        vmem((users, slots, half), BF16),
        vmem((CHUNKS, users, CORES * hist, LANES), BF16),
        vmem((CHUNKS, users, CORES * hist, LANES), BF16),
        vmem((YS, zs, 2 * SLOTS, LANES), F32),
        vmem((CHUNKS, YS, zs, 2 * SLOTS, LANES), BF16),
        vmem((CHUNKS, zs, 2 * SLOTS, LANES), F32),
        vmem((CHUNKS, YS - 1, zs, 2 * SLOTS, LANES), BF16),
        vmem((CHUNKS, 2 * SLOTS, LANES), F32),
        vmem((CHUNKS, zs, 2 * SLOTS, LANES), BF16),
        vmem((CHUNKS, zs - 1, 2 * SLOTS, LANES), BF16),
        vmem((CORES, CHUNKS, 2 * SLOTS, LANES), F32),
        vmem((users, entries, half), F32),
        vmem((2, 8, LANES), F32),
        vmem((YS - 1, 8, LANES), F32),
        vmem((zs - 1, 8, LANES), F32),
        vmem((2, 8, half), F32),
        dma((6,)),
        dma((CHUNKS,)),
        dma((2,)),
        dma((2,)),
        dma((2, 2, 2)),
        dma((2, 2, 2)),
        dma((2, 2)),
        dma((2, 2)),
        dma((2, 2, 2)),
        dma((2, 2, 2)),
        dma((zs - 1,)),
        dma((zs - 1,)),
        dma((1,)),
        dma((1,)),
        dma((1,)),
        dma((1,)),
        dma((1,)),
        dma((1,)),
        dma((2,)),
        dma((CHUNKS,)),
        dma((CHUNKS,)),
        dma((CHUNKS,)),
        dma((CHUNKS,)),
        dma((2,)),
        pltpu.SemaphoreType.REGULAR((zs // 2, 2)),
    ]
    vm = pl.BlockSpec(memory_space=pltpu.VMEM)
    scores, mixed, selt = pl.pallas_call(
        functools.partial(kernel, zs),
        out_shape=(
            jax.ShapeDtypeStruct((users, entries), F32),
            jax.ShapeDtypeStruct((2 * SLOTS, width), BF16),
            jax.ShapeDtypeStruct((users, entries, 2 * SLOTS), BF16),
        ),
        in_specs=[any_] * 6
        + [pl.BlockSpec(memory_space=pltpu.VMEM), pl.BlockSpec(memory_space=pltpu.SMEM)],
        out_specs=(vm, vm, vm),
        scratch_shapes=scratch,
        compiler_params=pltpu.CompilerParams(
            collective_id=0, has_side_effects=True, vmem_limit_bytes=56 * 1024 * 1024
        ),
        cost_estimate=pl.CostEstimate(
            flops=6_500_000_000, bytes_accessed=12_000_000, transcendentals=7_000_000
        ),
    )(memory, contenders, wc, wm, wco, avg, idx, ext)
    return pl.pallas_call(
        place_kernel,
        out_shape=(
            jax.ShapeDtypeStruct((users, entries), F32),
            jax.ShapeDtypeStruct((users, entries, width), BF16),
        ),
        in_specs=[vm, vm, vm],
        out_specs=(vm, vm),
    )(scores, mixed, selt)


def solution(mesh):
    placed = (
        P("user", "seq", None),
        P("user", "seq", None),
        P(),
        P(None, "user"),
        P(),
        P(),
        P("user", None),
        P("user"),
    )
    return jax.shard_map(
        local,
        mesh=mesh,
        in_specs=placed,
        out_specs=(P("user", "seq"), P("user", "seq", None)),
        check_vma=False,
    )
```
